32 devices in a mesh: vocab: 16 (over z, y, x), rows: 2 (over core).
Axes of the slice: x: 2, y: 2, z: 4, core: 2. Of those that a mesh axis runs over, the one named last changes fastest.
Arguments:
- hidden: bfloat16 [512, 4096], P('rows', 'vocab'), may hold values from -64 to 64
- head_weight: bfloat16 [4096, 16384], P(None, 'vocab'), may hold values from -0.09375 to 0.09375
- mentor_outputs: bfloat16 [512, 16384], P('rows', 'vocab'), may hold values from -480 to 480
Outputs:
- hidden_grad: bfloat16 [512, 4096], P('rows', 'vocab')
- weight_grad: bfloat16 [4096, 16384], P('rows', 'vocab')
- per_position_mismatch: float32 [512], P('rows')
The draws below stay inside these ranges and needn't reach their ends.
All inputs are finite; a program needn't handle non-finite values.
Results may differ from the reference program's by a relative error of at most 0.0043.
Values may be sent and summed in bfloat16 or wider, within the bound.
A program may use at most 128 MiB of HBM per device.

```python
import math
import jax
import jax.numpy as jnp

D = 4096
VOCAB = 16384
TOKENS = 512


def draw_hidden(key, part):
    key = jax.random.fold_in(key, 11)
    first, second = jax.random.split(key, 2)
    base = jnp.clip(jax.random.normal(first, (TOKENS, D), jnp.float32), -6.0, 6.0)
    scale = jnp.exp(jax.random.uniform(second, (TOKENS, 1), jnp.float32, 0.0, math.log(10.0)))
    return jnp.clip(base * scale, -64.0, 64.0).astype(jnp.bfloat16)


def draw_mentor_outputs(key, part):
    key = jax.random.fold_in(key, 12)
    first, second, third = jax.random.split(key, 3)
    column = jnp.arange(VOCAB, dtype=jnp.float32)[None, :] / VOCAB
    column_scale = (1.0 + 2.0 * column) * jnp.exp(jax.random.uniform(third, (1, VOCAB), jnp.float32, 0.0, math.log(2.0)))
    base = jnp.clip(jax.random.normal(first, (TOKENS, VOCAB), jnp.float32), -5.0, 5.0)
    scale = jnp.exp(jax.random.uniform(second, (TOKENS, 1), jnp.float32, 0.0, math.log(10.0)))
    return jnp.clip(base * scale * column_scale, -480.0, 480.0).astype(jnp.bfloat16)


def block_levels(own_key, shape, shards, smallest, high):
    gain, own = 1.0, jax.random.fold_in(own_key, 6)
    for position, parts in shards:
        draws = jnp.exp(jax.random.uniform(jax.random.fold_in(own, position), (parts,), jnp.float32, smallest / len(shards), high / len(shards)))
        gain = gain * jnp.repeat(draws, shape[position] // parts).reshape([-1 if axis == position else 1 for axis in range(len(shape))])
    return gain


def noise(own_key, dims, scale, bound, pieces=(), held_as=jnp.bfloat16):
    drawn = jax.random.normal(own_key, dims, jnp.float32) * scale
    if len(pieces) > 0:
        drawn = block_levels(own_key, dims, pieces, -0.22, 0.18) * drawn
    return jnp.clip(drawn, min=-bound, max=bound).astype(held_as)


def setup_inputs(seed: int = 0) -> dict:
    key_list = jax.random.split(jax.random.key(seed), 4)
    return {
        "hidden": draw_hidden(jax.random.fold_in(key_list[3], 71), 0),
        "head_weight": noise(key_list[1], (D, VOCAB), D ** -0.5, 0.09375, ((1, 16),)),
        "mentor_outputs": draw_mentor_outputs(jax.random.fold_in(key_list[3], 71), 0),
    }


sharpness_divisor = 2.0
objective_factor = 32.0


def reference(hidden, head_weight, mentor_outputs):
    unnormalized_outputs = jnp.dot(hidden, head_weight, preferred_element_type=jnp.float32)
    learner_raw_outputs = unnormalized_outputs / sharpness_divisor
    mentor_raw_outputs = mentor_outputs.astype(jnp.float32) / sharpness_divisor
    learner_partition_value = jax.nn.logsumexp(learner_raw_outputs, axis=1, keepdims=True)
    mentor_partition_value = jax.nn.logsumexp(mentor_raw_outputs, axis=1, keepdims=True)
    learner_likelihood = jnp.exp(learner_raw_outputs - learner_partition_value)
    mentor_likelihood = jnp.exp(mentor_raw_outputs - mentor_partition_value)
    mismatch_summand = jnp.sum(mentor_likelihood * (mentor_raw_outputs - learner_raw_outputs), axis=1)
    per_position_mismatch = sharpness_divisor * sharpness_divisor * (mismatch_summand + learner_partition_value[:, 0] - mentor_partition_value[:, 0])
    raw_score_derivative = (objective_factor * sharpness_divisor * (learner_likelihood - mentor_likelihood)).astype(jnp.bfloat16)
    hidden_grad = jnp.dot(raw_score_derivative, head_weight.T, preferred_element_type=jnp.float32).astype(jnp.bfloat16)
    weight_grad = jnp.dot(hidden.T, raw_score_derivative, preferred_element_type=jnp.float32).astype(jnp.bfloat16)
    return hidden_grad, weight_grad, per_position_mismatch
```

```python
import functools

import jax
import jax.numpy as jnp
from jax import lax
from jax.experimental import pallas as pl
from jax.experimental.pallas import tpu as pltpu
from jax.sharding import PartitionSpec as P

sharpness_divisor = 2.0
objective_factor = 32.0
f32 = jnp.float32
bf16 = jnp.bfloat16

NT = (((1,), (1,)), ((), ()))
TN = (((0,), (0,)), ((), ()))


def stages(h_hbm, w_hbm, t_hbm, hg_ref, wg_hbm, mm_ref,
           gath, pgath, w, t, es, et, score, pscore, cols, rowsbuf, stat,
           sa, ra, sb, rb, pb, q, sd, rd, wgs,
           loc_sem, ag_recv, z_send, xy_send, f_send, st_send, st_recv,
           a_send, a_recv, b_send, b_recv, d_send, d_recv, p_send, p_recv, out_sem):
    n = gath.shape[0]
    tok, width = h_hbm.shape
    half = tok // 2
    me = lax.axis_index("vocab")
    core = lax.axis_index("rows")
    z, y, x = me // 4, lax.rem(me // 2, 2), lax.rem(me, 2)
    mid = jnp.logical_or(z == 1, z == 2)

    def dev(zz, dy, dx):
        yy = 1 - y if dy else y
        xx = 1 - x if dx else x
        return zz * 4 + yy * 2 + xx

    z_near = z + 1 - 2 * lax.rem(z, 2)
    z_in = 3 - z
    low = z // 2
    planes = [z, z_near, 2 - low, 3 - 3 * low]
    xdev, ydev = dev(z, 0, 1), dev(z, 1, 0)

    def remote(src, dst, ss, rs, target):
        return pltpu.make_async_remote_copy(
            src_ref=src, dst_ref=dst, send_sem=ss, recv_sem=rs,
            device_id={"vocab": target}, device_id_type=pl.DeviceIdType.MESH)

    def partner(src, dst, i):
        return pltpu.make_async_remote_copy(
            src_ref=src, dst_ref=dst, send_sem=p_send.at[i], recv_sem=p_recv.at[i],
            device_id={"rows": 1 - core}, device_id_type=pl.DeviceIdType.MESH)

    cp_h = pltpu.make_async_copy(h_hbm, gath.at[me], loc_sem.at[0])
    cp_w = pltpu.make_async_copy(w_hbm, w, loc_sem.at[1])
    cp_t = pltpu.make_async_copy(t_hbm, t, loc_sem.at[2])
    cp_h.start()
    cp_t.start()
    cp_w.start()

    barrier = pltpu.get_barrier_semaphore()

    def greet(i, c):
        pl.semaphore_signal(barrier, inc=1, device_id={"vocab": lax.rem(me + i, n)},
                            device_id_type=pl.DeviceIdType.MESH)
        return c
    lax.fori_loop(1, n, greet, 0)
    pl.semaphore_signal(barrier, inc=1, device_id={"rows": 1 - core},
                        device_id_type=pl.DeviceIdType.MESH)
    pl.semaphore_wait(barrier, n)
    cp_h.wait()

    def piece(slot, h):
        return gath.at[slot, pl.ds(h * half, half)]

    def gcopy(slot, h, ss, target):
        return remote(piece(slot, h), piece(slot, h), ss, ag_recv.at[slot, h], target)

    def wait_piece(slot, h):
        gcopy(slot, h, f_send.at[0, 0], xdev).wait_recv()

    pending, pending_mid = [], []

    def go(c):
        c.start()
        pending.append(c)

    def go_mid(c):
        pl.when(mid)(c.start)
        pending_mid.append(c)

    def fan_out(i):
        slot = dev(planes[i], 0, 0)
        go(gcopy(slot, 0, xy_send.at[i, 0], ydev))
        go(gcopy(slot, 1, xy_send.at[i, 1], xdev))
        go(gcopy(slot, 1, xy_send.at[i, 2], ydev))
        go(gcopy(slot, 0, xy_send.at[i, 3], xdev))

    def forward(i):
        s0, s1 = dev(planes[i], 1, 0), dev(planes[i], 0, 1)
        wait_piece(s0, 0)
        go(gcopy(s0, 0, f_send.at[i, 0], xdev))
        wait_piece(s1, 1)
        go(gcopy(s1, 1, f_send.at[i, 1], ydev))

    def wrows(slot):
        return pl.ds(pl.multiple_of(slot * width, width), width)

    def multiply(slot, first=False):
        part = jnp.dot(gath[slot], w[wrows(slot), :], preferred_element_type=f32)
        if first:
            es[...] = part
        else:
            es[...] += part

    zn_dev, zi_dev = dev(z_near, 0, 0), dev(z_in, 0, 0)
    for h in range(2):
        go(gcopy(me, h, z_send.at[0, h], zn_dev))
        go_mid(gcopy(me, h, z_send.at[1, h], zi_dev))
    fan_out(0)

    block = 32
    nblk = tok // block
    lane = lax.broadcasted_iota(jnp.int32, (block, 128), 1)
    cp_t.wait()

    def teacher(b, c):
        rows = pl.ds(pl.multiple_of(b * block, block), block)
        tv = t[rows, :].astype(f32) / sharpness_divisor
        m = jnp.max(tv, axis=1, keepdims=True)
        e = jnp.exp(tv - m)
        et[rows, :] = e
        total = jnp.sum(e, axis=1, keepdims=True)
        cols[rows, :] = jnp.where(lane == 2, m, jnp.where(lane == 3, total, 0.0))
        return c
    lax.fori_loop(0, nblk, teacher, 0)

    cp_w.wait()
    multiply(me, True)
    for i in range(1, 4):
        slot = dev(planes[i], 0, 0)
        target = zi_dev if i == 1 else zn_dev
        for h in range(2):
            wait_piece(slot, h)
            go_mid(gcopy(slot, h, z_send.at[1 + i, h], target))
        fan_out(i)
        forward(i - 1)
        multiply(slot)
        if i > 1:
            s0, s1 = dev(planes[i - 2], 1, 0), dev(planes[i - 2], 0, 1)
            wait_piece(s0, 1)
            multiply(s0)
            wait_piece(s1, 0)
            multiply(s1)
    forward(3)
    for i in range(2):
        s = dev(planes[i], 1, 1)
        wait_piece(s, 0)
        wait_piece(s, 1)
        multiply(s)
    for i in range(2, 4):
        s0, s1, s = dev(planes[i], 1, 0), dev(planes[i], 0, 1), dev(planes[i], 1, 1)
        wait_piece(s0, 1)
        multiply(s0)
        wait_piece(s1, 0)
        multiply(s1)
        wait_piece(s, 0)
        wait_piece(s, 1)
        multiply(s)

    mine = n // 2
    ph = partner(gath.at[pl.ds((1 - core) * mine, mine)], pgath, 0)
    ph.start()

    def student(b, c):
        rows = pl.ds(pl.multiple_of(b * block, block), block)
        sv = es[rows, :] / sharpness_divisor
        tv = t[rows, :].astype(f32) / sharpness_divisor
        m = jnp.max(sv, axis=1, keepdims=True)
        e = jnp.exp(sv - m)
        es[rows, :] = e
        total = jnp.sum(e, axis=1, keepdims=True)
        weighted = jnp.sum(et[rows, :] * (tv - sv), axis=1, keepdims=True)
        old = cols[rows, :]
        cols[rows, :] = jnp.where(
            lane == 0, m, jnp.where(lane == 1, total, jnp.where(lane == 4, weighted, old)))
        return c
    lax.fori_loop(0, nblk, student, 0)
    stat[me] = jnp.transpose(cols[...])[:8, :]

    def stat_copy(i):
        return remote(stat.at[me], stat.at[me], st_send.at[i], st_recv.at[me],
                      lax.rem(me + i, n))

    def stat_start(i, c):
        stat_copy(i).start()
        return c
    lax.fori_loop(1, n, stat_start, 0)

    def stat_wait(i, c):
        other = lax.rem(me + i, n)
        remote(stat.at[other], stat.at[other], st_send.at[i], st_recv.at[other],
               other).wait_recv()
        return c
    lax.fori_loop(1, n, stat_wait, 0)

    ms, ss = stat[:, 0:1, :], stat[:, 1:2, :]
    mt, tt, wt = stat[:, 2:3, :], stat[:, 3:4, :], stat[:, 4:5, :]
    top_s, top_t = jnp.max(ms, axis=0), jnp.max(mt, axis=0)
    total_s = jnp.sum(ss * jnp.exp(ms - top_s[None]), axis=0)
    scale_t = jnp.exp(mt - top_t[None])
    total_t = jnp.sum(tt * scale_t, axis=0)
    cross = jnp.sum(wt * scale_t, axis=0) / total_t
    lse_s = top_s + jnp.log(total_s)
    lse_t = top_t + jnp.log(total_t)
    mm_ref[...] = sharpness_divisor * sharpness_divisor * (cross + lse_s - lse_t)
    own = stat[me]
    gain = objective_factor * sharpness_divisor
    rowsbuf[...] = jnp.zeros_like(rowsbuf)
    rowsbuf[0:1, :] = gain * jnp.exp(own[0:1, :] - lse_s)
    rowsbuf[1:2, :] = gain * jnp.exp(own[2:3, :] - lse_t)
    cols[...] = jnp.transpose(rowsbuf[...])

    def derive(b, c):
        rows = pl.ds(pl.multiple_of(b * block, block), block)
        f = cols[rows, :]
        score[rows, :] = (es[rows, :] * f[:, 0:1] - et[rows, :] * f[:, 1:2]).astype(bf16)
        return c
    lax.fori_loop(0, nblk, derive, 0)
    ps = partner(score, pscore, 1)
    ps.start()

    def part(slot):
        return lax.dot_general(score[...], w[wrows(slot), :], NT, preferred_element_type=f32)

    order = [planes[3], planes[2], planes[1], planes[0]]
    for k in range(4):
        p = part(dev(order[k], 1, 1)).astype(bf16)
        sa[k, 0] = p[:half]
        sa[k, 1] = p[half:]
        go(remote(sa.at[k, 0], ra.at[k, 0], a_send.at[k, 0], a_recv.at[k, 0], xdev))
        go(remote(sa.at[k, 1], ra.at[k, 1], a_send.at[k, 1], a_recv.at[k, 1], ydev))

    def bcopy(k, d, h):
        return remote(sb.at[k, d, h], rb.at[k, d, h], b_send.at[k, d, h],
                      b_recv.at[k, d, h], xdev if d else ydev)

    for k in range(4):
        p = part(dev(order[k], 1, 0))
        pb[k, 0] = p[:half]
        sb[k, 0, 1] = p[half:].astype(bf16)
        go(bcopy(k, 0, 1))
        p = part(dev(order[k], 0, 1))
        pb[k, 1] = p[half:]
        sb[k, 1, 0] = p[:half].astype(bf16)
        go(bcopy(k, 1, 0))
    for k in range(4):
        q[k] = part(dev(order[k], 0, 0))

    def weight_part(j, c):
        slot = core * mine + j
        for v in range(2):
            vs = pl.ds(v * (w.shape[1] // 2), w.shape[1] // 2)
            g = lax.dot_general(gath[slot], score[:, vs], TN, preferred_element_type=f32)
            g += lax.dot_general(pgath[j], pscore[:, vs], TN, preferred_element_type=f32)
            wgs[j, :, vs] = g.astype(bf16)
        pltpu.make_async_copy(wgs.at[j], wg_hbm.at[pl.ds(pl.multiple_of(j * width, width), width)],
                              out_sem.at[j]).start()
        return c

    def join(k):
        a = remote(sa.at[k, 0], ra.at[k, 0], a_send.at[k, 0], a_recv.at[k, 0], xdev)
        a.wait_recv()
        sb[k, 0, 0] = (pb[k, 0] + ra[k, 0].astype(f32)).astype(bf16)
        go(bcopy(k, 0, 0))
        a = remote(sa.at[k, 1], ra.at[k, 1], a_send.at[k, 1], a_recv.at[k, 1], ydev)
        a.wait_recv()
        sb[k, 1, 1] = (pb[k, 1] + ra[k, 1].astype(f32)).astype(bf16)
        go(bcopy(k, 1, 1))

    join(0)
    join(1)
    ph.wait()
    ps.wait()
    lax.fori_loop(0, mine // 2, weight_part, 0)
    join(2)
    join(3)
    lax.fori_loop(mine // 2, mine, weight_part, 0)

    for k in range(4):
        for d in range(2):
            for h in range(2):
                bcopy(k, d, h).wait_recv()
        for h in range(2):
            hs = pl.ds(h * half, half)
            q[k, hs, :] += rb[k, 0, h].astype(f32) + rb[k, 1, h].astype(f32)
        if k < 3:
            sd[k] = q[k].astype(bf16)
            go(remote(sd.at[k], rd.at[z], d_send.at[k], d_recv.at[z], dev(order[k], 0, 0)))
    total = q[3]
    for k in range(3):
        zz = order[k]
        remote(sd.at[k], rd.at[zz], d_send.at[k], d_recv.at[zz], dev(zz, 0, 0)).wait_recv()
        total += rd[zz].astype(f32)
    hg_ref[...] = total.astype(bf16)

    for c in pending:
        c.wait_send()

    @pl.when(mid)
    def _():
        for c in pending_mid:
            c.wait_send()

    def stat_done(i, c):
        stat_copy(i).wait_send()
        return c
    lax.fori_loop(1, n, stat_done, 0)

    def out_done(j, c):
        pltpu.make_async_copy(wgs.at[j], wg_hbm.at[pl.ds(pl.multiple_of(j * width, width), width)],
                              out_sem.at[j]).wait()
        return c
    lax.fori_loop(0, mine, out_done, 0)


def fused(n, hidden, head_weight, mentor_outputs):
    tok, width = hidden.shape
    feats, voc = head_weight.shape
    half, mine = tok // 2, n // 2
    vm = pltpu.VMEM
    dma = pltpu.SemaphoreType.DMA
    anyspace = pl.BlockSpec(memory_space=pl.ANY)
    vspace = pl.BlockSpec(memory_space=pltpu.VMEM)
    hg, wg, mm = pl.pallas_call(
        stages,
        out_shape=(
            jax.ShapeDtypeStruct((tok, width), bf16),
            jax.ShapeDtypeStruct((feats // 2, voc), bf16),
            jax.ShapeDtypeStruct((1, tok), f32),
        ),
        in_specs=[anyspace] * 3,
        out_specs=(vspace, anyspace, vspace),
        scratch_shapes=[
            vm((n, tok, width), bf16),
            vm((mine, tok, width), bf16),
            vm((feats, voc), bf16),
            vm((tok, voc), bf16),
            vm((tok, voc), f32),
            vm((tok, voc), f32),
            vm((tok, voc), bf16),
            vm((tok, voc), bf16),
            vm((tok, 128), f32),
            vm((128, tok), f32),
            vm((n, 8, tok), f32),
            vm((4, 2, half, width), bf16),
            vm((4, 2, half, width), bf16),
            vm((4, 2, 2, half, width), bf16),
            vm((4, 2, 2, half, width), bf16),
            vm((4, 2, half, width), f32),
            vm((4, tok, width), f32),
            vm((3, tok, width), bf16),
            vm((4, tok, width), bf16),
            vm((mine, width, voc), bf16),
            dma((3,)),
            dma((n, 2)),
            dma((5, 2)),
            dma((4, 4)),
            dma((4, 2)),
            dma((n,)),
            dma((n,)),
            dma((4, 2)),
            dma((4, 2)),
            dma((4, 2, 2)),
            dma((4, 2, 2)),
            dma((3,)),
            dma((4,)),
            dma((2,)),
            dma((2,)),
            dma((mine,)),
        ],
        compiler_params=pltpu.CompilerParams(
            collective_id=0, has_side_effects=True, vmem_limit_bytes=48 * 1024 * 1024),
        cost_estimate=pl.CostEstimate(
            flops=6 * tok * feats * voc, transcendentals=2 * tok * voc,
            bytes_accessed=2 * feats * voc + feats * voc),
    )(hidden, head_weight, mentor_outputs)
    return hg, wg, mm.reshape(tok)


def collective(hidden, head_weight, mentor_outputs):
    full_hidden = lax.all_gather(hidden, "vocab", axis=1, tiled=True)
    student = jnp.dot(full_hidden, head_weight, preferred_element_type=f32) / sharpness_divisor
    target = mentor_outputs.astype(f32) / sharpness_divisor
    top_s, top_t = lax.pmax((jnp.max(student, axis=1), jnp.max(target, axis=1)), "vocab")
    exp_s = jnp.exp(student - top_s[:, None])
    exp_t = jnp.exp(target - top_t[:, None])
    total_s, total_t, weighted = lax.psum(
        (jnp.sum(exp_s, axis=1), jnp.sum(exp_t, axis=1),
         jnp.sum(exp_t * (target - student), axis=1)), "vocab")
    lse_s = top_s + jnp.log(total_s)
    lse_t = top_t + jnp.log(total_t)
    mismatch = sharpness_divisor * sharpness_divisor * (weighted / total_t + lse_s - lse_t)
    score = (objective_factor * sharpness_divisor
             * (jnp.exp(student - lse_s[:, None]) - jnp.exp(target - lse_t[:, None]))).astype(bf16)
    hidden_part = lax.psum_scatter(
        lax.dot_general(head_weight, score, NT, preferred_element_type=f32),
        "vocab", scatter_dimension=0, tiled=True)
    weight_grad = lax.psum_scatter(
        lax.dot_general(full_hidden, score, TN, preferred_element_type=f32),
        "rows", scatter_dimension=0, tiled=True).astype(bf16)
    return hidden_part.T.astype(bf16), weight_grad, mismatch


def solution(mesh):
    n = mesh.shape["vocab"]

    def shards(hidden, head_weight, mentor_outputs):
        if n == 16 and mesh.shape["rows"] == 2 and hidden.shape[1] % 128 == 0:
            return fused(n, hidden, head_weight, mentor_outputs)
        return collective(hidden, head_weight, mentor_outputs)

    return jax.shard_map(
        shards,
        mesh=mesh,
        in_specs=(P("rows", "vocab"), P(None, "vocab"), P("rows", "vocab")),
        out_specs=(P("rows", "vocab"), P("rows", "vocab"), P("rows")),
        check_vma=False,
    )
```

```python
import functools

import jax
import jax.numpy as jnp
from jax import lax
from jax.experimental import pallas as pl
from jax.experimental.pallas import tpu as pltpu
from jax.sharding import PartitionSpec as P

sharpness_divisor = 2.0
objective_factor = 32.0
f32 = jnp.float32
bf16 = jnp.bfloat16

NT = (((1,), (1,)), ((), ()))
TN = (((0,), (0,)), ((), ()))
BATCHES = 2


def stages(h_hbm, w_hbm, t_hbm, hg_ref, wg_hbm, mm_ref,
           gath, pgath, w, t, es, et, score, pscore, cols, rowsbuf, stat,
           sa, ra, sb, rb, pb, q, sd, rd, wgs,
           loc_sem, ag_recv, z_send, xy_send, f_send, st_send, st_recv,
           a_send, a_recv, b_send, b_recv, d_send, d_recv, p_send, p_recv, out_sem):
    n = gath.shape[0]
    tok, width = h_hbm.shape
    batch = tok // BATCHES
    half = batch // 2
    me = lax.axis_index("vocab")
    core = lax.axis_index("rows")
    z, y, x = me // 4, lax.rem(me // 2, 2), lax.rem(me, 2)
    mid = jnp.logical_or(z == 1, z == 2)

    def dev(zz, dy, dx):
        yy = 1 - y if dy else y
        xx = 1 - x if dx else x
        return zz * 4 + yy * 2 + xx

    z_near = z + 1 - 2 * lax.rem(z, 2)
    z_in = 3 - z
    low = z // 2
    planes = [z, z_near, 2 - low, 3 - 3 * low]
    order = planes[::-1]
    xdev, ydev = dev(z, 0, 1), dev(z, 1, 0)
    zn_dev, zi_dev = dev(z_near, 0, 0), dev(z_in, 0, 0)

    def remote(src, dst, ss, rs, target):
        return pltpu.make_async_remote_copy(
            src_ref=src, dst_ref=dst, send_sem=ss, recv_sem=rs,
            device_id={"vocab": target}, device_id_type=pl.DeviceIdType.MESH)

    def partner(src, dst, i):
        return pltpu.make_async_remote_copy(
            src_ref=src, dst_ref=dst, send_sem=p_send.at[i], recv_sem=p_recv.at[i],
            device_id={"rows": 1 - core}, device_id_type=pl.DeviceIdType.MESH)

    cp_h = pltpu.make_async_copy(h_hbm, gath.at[me], loc_sem.at[0])
    cp_w = pltpu.make_async_copy(w_hbm, w, loc_sem.at[1])
    cp_t = pltpu.make_async_copy(t_hbm, t, loc_sem.at[2])
    cp_h.start()
    cp_t.start()
    cp_w.start()

    barrier = pltpu.get_barrier_semaphore()

    def greet(i, c):
        pl.semaphore_signal(barrier, inc=1, device_id={"vocab": lax.rem(me + i, n)},
                            device_id_type=pl.DeviceIdType.MESH)
        return c
    lax.fori_loop(1, n, greet, 0)
    pl.semaphore_signal(barrier, inc=1, device_id={"rows": 1 - core},
                        device_id_type=pl.DeviceIdType.MESH)
    pl.semaphore_wait(barrier, n)
    cp_h.wait()

    pending, pending_mid = [], []

    def go(c):
        c.start()
        pending.append(c)

    def go_mid(c):
        pl.when(mid)(c.start)
        pending_mid.append(c)

    def gcopy(b, slot, h, ss, target):
        ref = gath.at[slot, pl.ds(b * batch + h * half, half)]
        return remote(ref, ref, ss, ag_recv.at[slot, b, h], target)

    def wait_piece(b, slot, h):
        gcopy(b, slot, h, f_send.at[b, 0, 0], xdev).wait_recv()

    def z_start(b):
        for h in range(2):
            go(gcopy(b, me, h, z_send.at[b, 0, h], zn_dev))
            go_mid(gcopy(b, me, h, z_send.at[b, 1, h], zi_dev))

    def z_step(b, i):
        slot = dev(planes[i], 0, 0)
        for h in range(2):
            wait_piece(b, slot, h)
            go_mid(gcopy(b, slot, h, z_send.at[b, 1 + i, h], zi_dev if i == 1 else zn_dev))

    def fan_out(b, i):
        slot = dev(planes[i], 0, 0)
        go(gcopy(b, slot, 0, xy_send.at[b, i, 0], ydev))
        go(gcopy(b, slot, 1, xy_send.at[b, i, 1], xdev))
        go(gcopy(b, slot, 1, xy_send.at[b, i, 2], ydev))
        go(gcopy(b, slot, 0, xy_send.at[b, i, 3], xdev))

    def forward(b, i):
        s0, s1 = dev(planes[i], 1, 0), dev(planes[i], 0, 1)
        wait_piece(b, s0, 0)
        go(gcopy(b, s0, 0, f_send.at[b, i, 0], xdev))
        wait_piece(b, s1, 1)
        go(gcopy(b, s1, 1, f_send.at[b, i, 1], ydev))

    def wrows(slot):
        return pl.ds(pl.multiple_of(slot * width, width), width)

    def brows(b):
        return pl.ds(b * batch, batch)

    def multiply(b, slot, first=False):
        part = jnp.dot(gath[slot, brows(b), :], w[wrows(slot), :], preferred_element_type=f32)
        if first:
            es[brows(b), :] = part
        else:
            es[brows(b), :] += part

    def sides(b, i):
        s0, s1 = dev(planes[i], 1, 0), dev(planes[i], 0, 1)
        wait_piece(b, s0, 1)
        multiply(b, s0)
        wait_piece(b, s1, 0)
        multiply(b, s1)

    def diagonal(b, i):
        s = dev(planes[i], 1, 1)
        wait_piece(b, s, 0)
        wait_piece(b, s, 1)
        multiply(b, s)

    block = 32
    nblk = batch // block
    lane = lax.broadcasted_iota(jnp.int32, (block, 128), 1)

    def teacher(i, c):
        rows = pl.ds(pl.multiple_of(i * block, block), block)
        tv = t[rows, :].astype(f32) / sharpness_divisor
        m = jnp.max(tv, axis=1, keepdims=True)
        e = jnp.exp(tv - m)
        et[rows, :] = e
        total = jnp.sum(e, axis=1, keepdims=True)
        cols[rows, :] = jnp.where(lane == 2, m, jnp.where(lane == 3, total, 0.0))
        return c

    def student(i, c):
        rows = pl.ds(pl.multiple_of(i * block, block), block)
        sv = es[rows, :] / sharpness_divisor
        tv = t[rows, :].astype(f32) / sharpness_divisor
        m = jnp.max(sv, axis=1, keepdims=True)
        e = jnp.exp(sv - m)
        es[rows, :] = e
        total = jnp.sum(e, axis=1, keepdims=True)
        weighted = jnp.sum(et[rows, :] * (tv - sv), axis=1, keepdims=True)
        old = cols[rows, :]
        cols[rows, :] = jnp.where(
            lane == 0, m, jnp.where(lane == 1, total, jnp.where(lane == 4, weighted, old)))
        return c

    def stat_copy(b, i):
        return remote(stat.at[b, me], stat.at[b, me], st_send.at[b, i], st_recv.at[b, me],
                      lax.rem(me + i, n))

    def stat_send(b):
        lax.fori_loop(b * nblk, (b + 1) * nblk, student, 0)
        stat[b, me] = jnp.transpose(cols[brows(b), :])[:8, :]

        def start(i, c):
            stat_copy(b, i).start()
            return c
        lax.fori_loop(1, n, start, 0)

    def derive(i, c):
        rows = pl.ds(pl.multiple_of(i * block, block), block)
        f = cols[rows, :]
        score[rows, :] = (es[rows, :] * f[:, 0:1] - et[rows, :] * f[:, 1:2]).astype(bf16)
        return c

    def stat_join(b):
        def wait(i, c):
            other = lax.rem(me + i, n)
            remote(stat.at[b, other], stat.at[b, other], st_send.at[b, i],
                   st_recv.at[b, other], other).wait_recv()
            return c
        lax.fori_loop(1, n, wait, 0)
        ms, ss = stat[b, :, 0:1, :], stat[b, :, 1:2, :]
        mt, tt, wt = stat[b, :, 2:3, :], stat[b, :, 3:4, :], stat[b, :, 4:5, :]
        top_s, top_t = jnp.max(ms, axis=0), jnp.max(mt, axis=0)
        total_s = jnp.sum(ss * jnp.exp(ms - top_s[None]), axis=0)
        scale_t = jnp.exp(mt - top_t[None])
        total_t = jnp.sum(tt * scale_t, axis=0)
        cross = jnp.sum(wt * scale_t, axis=0) / total_t
        lse_s = top_s + jnp.log(total_s)
        lse_t = top_t + jnp.log(total_t)
        mm_ref[:, brows(b)] = sharpness_divisor * sharpness_divisor * (cross + lse_s - lse_t)
        own = stat[b, me]
        gain = objective_factor * sharpness_divisor
        rowsbuf[b, 0:1, :] = gain * jnp.exp(own[0:1, :] - lse_s)
        rowsbuf[b, 1:2, :] = gain * jnp.exp(own[2:3, :] - lse_t)
        cols[brows(b), :] = jnp.transpose(rowsbuf[b])
        lax.fori_loop(b * nblk, (b + 1) * nblk, derive, 0)

    def part(b, slot):
        return lax.dot_general(score[brows(b), :], w[wrows(slot), :], NT,
                               preferred_element_type=f32)

    def acopy(b, k, h):
        return remote(sa.at[b, k, h], ra.at[b, k, h], a_send.at[b, k, h],
                      a_recv.at[b, k, h], ydev if h else xdev)

    def bcopy(b, k, d, h):
        return remote(sb.at[b, k, d, h], rb.at[b, k, d, h], b_send.at[b, k, d, h],
                      b_recv.at[b, k, d, h], xdev if d else ydev)

    def spread(b):
        for k in range(4):
            p = part(b, dev(order[k], 1, 1)).astype(bf16)
            sa[b, k, 0] = p[:half]
            sa[b, k, 1] = p[half:]
            go(acopy(b, k, 0))
            go(acopy(b, k, 1))
        for k in range(4):
            p = part(b, dev(order[k], 1, 0))
            pb[b, k, 0] = p[:half]
            sb[b, k, 0, 1] = p[half:].astype(bf16)
            go(bcopy(b, k, 0, 1))
            p = part(b, dev(order[k], 0, 1))
            pb[b, k, 1] = p[half:]
            sb[b, k, 1, 0] = p[:half].astype(bf16)
            go(bcopy(b, k, 1, 0))

    def home(b):
        for k in range(4):
            q[b, k] = part(b, dev(order[k], 0, 0))

    def join(b, k):
        acopy(b, k, 0).wait_recv()
        sb[b, k, 0, 0] = (pb[b, k, 0] + ra[b, k, 0].astype(f32)).astype(bf16)
        go(bcopy(b, k, 0, 0))
        acopy(b, k, 1).wait_recv()
        sb[b, k, 1, 1] = (pb[b, k, 1] + ra[b, k, 1].astype(f32)).astype(bf16)
        go(bcopy(b, k, 1, 1))

    def column(b, k):
        for d in range(2):
            for h in range(2):
                bcopy(b, k, d, h).wait_recv()
        for h in range(2):
            hs = pl.ds(h * half, half)
            q[b, k, hs, :] += rb[b, k, 0, h].astype(f32) + rb[b, k, 1, h].astype(f32)
        if k < 3:
            sd[b, k] = q[b, k].astype(bf16)
            go(remote(sd.at[b, k], rd.at[b, z], d_send.at[b, k], d_recv.at[b, z],
                      dev(order[k], 0, 0)))

    def finish(b):
        total = q[b, 3]
        for k in range(3):
            zz = order[k]
            remote(sd.at[b, k], rd.at[b, zz], d_send.at[b, k], d_recv.at[b, zz],
                   dev(zz, 0, 0)).wait_recv()
            total += rd[b, zz].astype(f32)
        hg_ref[brows(b), :] = total.astype(bf16)

    mine = n // 2

    def out_copy(j):
        return pltpu.make_async_copy(
            wgs.at[j], wg_hbm.at[pl.ds(pl.multiple_of(j * width, width), width)], out_sem.at[j])

    def weight_part(j, c):
        slot = core * mine + j
        for v in range(2):
            vs = pl.ds(v * (w.shape[1] // 2), w.shape[1] // 2)
            g = lax.dot_general(gath[slot], score[:, vs], TN, preferred_element_type=f32)
            g += lax.dot_general(pgath[j], pscore[:, vs], TN, preferred_element_type=f32)
            wgs[j, :, vs] = g.astype(bf16)
        out_copy(j).start()
        return c

    z_start(0)
    fan_out(0, 0)
    z_start(1)
    rowsbuf[...] = jnp.zeros_like(rowsbuf)
    cp_t.wait()
    lax.fori_loop(0, BATCHES * nblk, teacher, 0)
    cp_w.wait()
    multiply(0, me, True)
    for i in range(1, 4):
        z_step(0, i)
        fan_out(0, i)
        z_step(1, i)
        forward(0, i - 1)
        multiply(0, dev(planes[i], 0, 0))
        if i > 1:
            sides(0, i - 2)
    forward(0, 3)
    for i in range(4):
        fan_out(1, i)
    diagonal(0, 0)
    diagonal(0, 1)
    forward(1, 0)
    sides(0, 2)
    diagonal(0, 2)
    sides(0, 3)
    diagonal(0, 3)
    stat_send(0)
    forward(1, 1)
    multiply(1, me, True)
    multiply(1, dev(planes[1], 0, 0))
    sides(1, 0)
    forward(1, 2)
    stat_join(0)
    forward(1, 3)
    spread(0)
    multiply(1, dev(planes[2], 0, 0))
    multiply(1, dev(planes[3], 0, 0))
    for i in range(4):
        if i:
            sides(1, i)
        diagonal(1, i)
    ph = partner(gath.at[pl.ds((1 - core) * mine, mine)], pgath, 0)
    ph.start()
    stat_send(1)
    for k in range(4):
        join(0, k)
    home(0)
    stat_join(1)
    ps = partner(score, pscore, 1)
    ps.start()
    spread(1)
    for k in range(4):
        column(0, k)
    home(1)
    join(1, 0)
    join(1, 1)
    ph.wait()
    ps.wait()
    lax.fori_loop(0, mine // 2, weight_part, 0)
    join(1, 2)
    join(1, 3)
    finish(0)
    lax.fori_loop(mine // 2, mine, weight_part, 0)
    for k in range(4):
        column(1, k)
    finish(1)

    for c in pending:
        c.wait_send()

    @pl.when(mid)
    def _():
        for c in pending_mid:
            c.wait_send()

    def stat_done(i, c):
        for b in range(BATCHES):
            stat_copy(b, i).wait_send()
        return c
    lax.fori_loop(1, n, stat_done, 0)

    def out_done(j, c):
        out_copy(j).wait()
        return c
    lax.fori_loop(0, mine, out_done, 0)


def publish(*refs):
    k = len(refs) // 2
    sems = refs[-1]
    copies = [pltpu.make_async_copy(refs[i], refs[k + i], sems.at[i]) for i in range(k)]
    for c in copies:
        c.start()
    for c in copies:
        c.wait()


def fused(n, hidden, head_weight, mentor_outputs):
    tok, width = hidden.shape
    feats, voc = head_weight.shape
    batch, mine = tok // BATCHES, n // 2
    half = batch // 2
    nb = BATCHES
    vm = pltpu.VMEM
    dma = pltpu.SemaphoreType.DMA
    anyspace = pl.BlockSpec(memory_space=pl.ANY)
    vspace = pl.BlockSpec(memory_space=pltpu.VMEM)
    hbm = pl.BlockSpec(memory_space=pltpu.HBM)
    shapes = (
        jax.ShapeDtypeStruct((tok, width), bf16),
        jax.ShapeDtypeStruct((feats // 2, voc), bf16),
        jax.ShapeDtypeStruct((1, tok), f32),
    )
    made = pl.pallas_call(
        stages,
        out_shape=shapes,
        in_specs=[hbm] * 3,
        out_specs=(vspace, anyspace, vspace),
        scratch_shapes=[
            vm((n, tok, width), bf16),
            vm((mine, tok, width), bf16),
            vm((feats, voc), bf16),
            vm((tok, voc), bf16),
            vm((tok, voc), f32),
            vm((tok, voc), f32),
            vm((tok, voc), bf16),
            vm((tok, voc), bf16),
            vm((tok, 128), f32),
            vm((nb, 128, batch), f32),
            vm((nb, n, 8, batch), f32),
            vm((nb, 4, 2, half, width), bf16),
            vm((nb, 4, 2, half, width), bf16),
            vm((nb, 4, 2, 2, half, width), bf16),
            vm((nb, 4, 2, 2, half, width), bf16),
            vm((nb, 4, 2, half, width), f32),
            vm((nb, 4, batch, width), f32),
            vm((nb, 3, batch, width), bf16),
            vm((nb, 4, batch, width), bf16),
            vm((mine, width, voc), bf16),
            dma((3,)),
            dma((n, nb, 2)),
            dma((nb, 5, 2)),
            dma((nb, 4, 4)),
            dma((nb, 4, 2)),
            dma((nb, n)),
            dma((nb, n)),
            dma((nb, 4, 2)),
            dma((nb, 4, 2)),
            dma((nb, 4, 2, 2)),
            dma((nb, 4, 2, 2)),
            dma((nb, 3)),
            dma((nb, 4)),
            dma((2,)),
            dma((2,)),
            dma((mine,)),
        ],
        compiler_params=pltpu.CompilerParams(
            collective_id=0, has_side_effects=True, vmem_limit_bytes=48 * 1024 * 1024),
        cost_estimate=pl.CostEstimate(
            flops=6 * tok * feats * voc, transcendentals=2 * tok * voc,
            bytes_accessed=2 * feats * voc + feats * voc),
    )(hidden, head_weight, mentor_outputs)
    hg, wg, mm = pl.pallas_call(
        publish,
        out_shape=shapes,
        in_specs=[anyspace] * 3,
        out_specs=(hbm,) * 3,
        scratch_shapes=[dma((3,))],
    )(*made)
    return hg, wg, mm.reshape(tok)


def collective(hidden, head_weight, mentor_outputs):
    full_hidden = lax.all_gather(hidden, "vocab", axis=1, tiled=True)
    student = jnp.dot(full_hidden, head_weight, preferred_element_type=f32) / sharpness_divisor
    target = mentor_outputs.astype(f32) / sharpness_divisor
    top_s, top_t = lax.pmax((jnp.max(student, axis=1), jnp.max(target, axis=1)), "vocab")
    exp_s = jnp.exp(student - top_s[:, None])
    exp_t = jnp.exp(target - top_t[:, None])
    total_s, total_t, weighted = lax.psum(
        (jnp.sum(exp_s, axis=1), jnp.sum(exp_t, axis=1),
         jnp.sum(exp_t * (target - student), axis=1)), "vocab")
    lse_s = top_s + jnp.log(total_s)
    lse_t = top_t + jnp.log(total_t)
    mismatch = sharpness_divisor * sharpness_divisor * (weighted / total_t + lse_s - lse_t)
    score = (objective_factor * sharpness_divisor
             * (jnp.exp(student - lse_s[:, None]) - jnp.exp(target - lse_t[:, None]))).astype(bf16)
    hidden_part = lax.psum_scatter(
        lax.dot_general(head_weight, score, NT, preferred_element_type=f32),
        "vocab", scatter_dimension=0, tiled=True)
    weight_grad = lax.psum_scatter(
        lax.dot_general(full_hidden, score, TN, preferred_element_type=f32),
        "rows", scatter_dimension=0, tiled=True).astype(bf16)
    return hidden_part.T.astype(bf16), weight_grad, mismatch


def solution(mesh):
    n = mesh.shape["vocab"]

    def shards(hidden, head_weight, mentor_outputs):
        if n == 16 and mesh.shape["rows"] == 2 and hidden.shape[1] % 128 == 0:
            return fused(n, hidden, head_weight, mentor_outputs)
        return collective(hidden, head_weight, mentor_outputs)

    return jax.shard_map(
        shards,
        mesh=mesh,
        in_specs=(P("rows", "vocab"), P(None, "vocab"), P("rows", "vocab")),
        out_specs=(P("rows", "vocab"), P("rows", "vocab"), P("rows")),
        check_vma=False,
    )
```

```python
import functools

import jax
import jax.numpy as jnp
from jax import lax
from jax.experimental import pallas as pl
from jax.experimental.pallas import tpu as pltpu
from jax.sharding import PartitionSpec as P

sharpness_divisor = 2.0
objective_factor = 32.0
f32 = jnp.float32
bf16 = jnp.bfloat16

NT = (((1,), (1,)), ((), ()))
TN = (((0,), (0,)), ((), ()))


def stages(h_ref, w_hbm, t, hg_ref, wg_ref, mm_ref,
           gath, pgath, w, es, et, score, cols, rowsbuf, stat,
           sa, ra, sb, rb, pp, sd, rd,
           loc_sem, ag_recv, z_send, xy_send, f_send, st_send, st_recv,
           a_send, a_recv, b_send, b_recv, d_send, d_recv, p_send, p_recv):
    n = gath.shape[0]
    tok, width = h_ref.shape
    half = tok // 2
    me = lax.axis_index("vocab")
    core = lax.axis_index("rows")
    z, y, x = me // 4, lax.rem(me // 2, 2), lax.rem(me, 2)
    mid = jnp.logical_or(z == 1, z == 2)

    def dev(zz, dy, dx):
        yy = 1 - y if dy else y
        xx = 1 - x if dx else x
        return zz * 4 + yy * 2 + xx

    z_near = z + 1 - 2 * lax.rem(z, 2)
    z_in = 3 - z
    low = z // 2
    planes = [z, z_near, 2 - low, 3 - 3 * low]
    xdev, ydev = dev(z, 0, 1), dev(z, 1, 0)

    def remote(src, dst, ss, rs, target):
        return pltpu.make_async_remote_copy(
            src_ref=src, dst_ref=dst, send_sem=ss, recv_sem=rs,
            device_id={"vocab": target}, device_id_type=pl.DeviceIdType.MESH)

    def partner(src, dst, i):
        return pltpu.make_async_remote_copy(
            src_ref=src, dst_ref=dst, send_sem=p_send.at[i], recv_sem=p_recv.at[i],
            device_id={"rows": 1 - core}, device_id_type=pl.DeviceIdType.MESH)

    cp_w = pltpu.make_async_copy(w_hbm, w, loc_sem.at[0])
    cp_w.start()
    gath[me] = h_ref[...]

    barrier = pltpu.get_barrier_semaphore()

    def greet(i, c):
        pl.semaphore_signal(barrier, inc=1, device_id={"vocab": lax.rem(me + i, n)},
                            device_id_type=pl.DeviceIdType.MESH)
        return c
    lax.fori_loop(1, n, greet, 0)
    pl.semaphore_signal(barrier, inc=1, device_id={"rows": 1 - core},
                        device_id_type=pl.DeviceIdType.MESH)
    pl.semaphore_wait(barrier, n)

    def piece(slot, h):
        return gath.at[slot, pl.ds(h * half, half)]

    def gcopy(slot, h, ss, target):
        return remote(piece(slot, h), piece(slot, h), ss, ag_recv.at[slot, h], target)

    def wait_piece(slot, h):
        gcopy(slot, h, f_send.at[0, 0], xdev).wait_recv()

    pending, pending_mid = [], []

    def go(c):
        c.start()
        pending.append(c)

    def go_mid(c):
        pl.when(mid)(c.start)
        pending_mid.append(c)

    def fan_out(i):
        slot = dev(planes[i], 0, 0)
        go(gcopy(slot, 0, xy_send.at[i, 0], ydev))
        go(gcopy(slot, 1, xy_send.at[i, 1], xdev))
        go(gcopy(slot, 1, xy_send.at[i, 2], ydev))
        go(gcopy(slot, 0, xy_send.at[i, 3], xdev))

    def forward(i):
        s0, s1 = dev(planes[i], 1, 0), dev(planes[i], 0, 1)
        wait_piece(s0, 0)
        go(gcopy(s0, 0, f_send.at[i, 0], xdev))
        wait_piece(s1, 1)
        go(gcopy(s1, 1, f_send.at[i, 1], ydev))

    def wrows(slot, count):
        return pl.ds(pl.multiple_of(slot * width, width), count * width)

    def multiply(slot, count, first=False):
        a = jnp.concatenate([gath[slot + c] for c in range(count)], axis=1)
        part = jnp.dot(a, w[wrows(slot, count), :], preferred_element_type=f32)
        if first:
            es[...] = part
        else:
            es[...] += part

    def plane(i):
        s0, s1, s = dev(planes[i], 1, 0), dev(planes[i], 0, 1), dev(planes[i], 1, 1)
        wait_piece(s0, 1)
        wait_piece(s1, 0)
        if i == 3:
            multiply(planes[3] * 4 + 2 * y, 2)
        wait_piece(s, 0)
        wait_piece(s, 1)
        if i == 3:
            multiply(planes[3] * 4 + 2 * (1 - y), 2)
        else:
            multiply(planes[i] * 4, 4, i == 0)

    zn_dev, zi_dev = dev(z_near, 0, 0), dev(z_in, 0, 0)
    for h in range(2):
        go(gcopy(me, h, z_send.at[0, h], zn_dev))
        go_mid(gcopy(me, h, z_send.at[1, h], zi_dev))
    fan_out(0)

    block = 32
    nblk = tok // block
    lane = lax.broadcasted_iota(jnp.int32, (block, 128), 1)

    def teacher(b, c):
        rows = pl.ds(pl.multiple_of(b * block, block), block)
        tv = t[rows, :].astype(f32) / sharpness_divisor
        m = jnp.max(tv, axis=1, keepdims=True)
        e = jnp.exp(tv - m)
        et[rows, :] = e
        total = jnp.sum(e, axis=1, keepdims=True)
        cols[rows, :] = jnp.where(lane == 2, m, jnp.where(lane == 3, total, 0.0))
        return c
    lax.fori_loop(0, nblk, teacher, 0)

    for i in range(1, 4):
        slot = dev(planes[i], 0, 0)
        target = zi_dev if i == 1 else zn_dev
        for h in range(2):
            wait_piece(slot, h)
            go_mid(gcopy(slot, h, z_send.at[1 + i, h], target))
        fan_out(i)
        forward(i - 1)
        if i > 1:
            if i == 2:
                cp_w.wait()
            plane(i - 2)
    forward(3)
    plane(2)
    plane(3)

    mine = n // 2
    ph = partner(gath.at[pl.ds((1 - core) * mine, mine)], pgath, 0)
    ph.start()

    def student(b, c):
        rows = pl.ds(pl.multiple_of(b * block, block), block)
        sv = es[rows, :] / sharpness_divisor
        tv = t[rows, :].astype(f32) / sharpness_divisor
        m = jnp.max(sv, axis=1, keepdims=True)
        e = jnp.exp(sv - m)
        es[rows, :] = e
        total = jnp.sum(e, axis=1, keepdims=True)
        weighted = jnp.sum(et[rows, :] * (tv - sv), axis=1, keepdims=True)
        old = cols[rows, :]
        cols[rows, :] = jnp.where(
            lane == 0, m, jnp.where(lane == 1, total, jnp.where(lane == 4, weighted, old)))
        return c
    lax.fori_loop(0, nblk, student, 0)
    stat[me] = jnp.transpose(cols[...])[:8, :]

    def stat_copy(i):
        return remote(stat.at[me], stat.at[me], st_send.at[i], st_recv.at[me],
                      lax.rem(me + i, n))

    def stat_start(i, c):
        stat_copy(i).start()
        return c
    lax.fori_loop(1, n, stat_start, 0)

    def stat_wait(i, c):
        other = lax.rem(me + i, n)
        remote(stat.at[other], stat.at[other], st_send.at[i], st_recv.at[other],
               other).wait_recv()
        return c
    lax.fori_loop(1, n, stat_wait, 0)

    ms, ss = stat[:, 0:1, :], stat[:, 1:2, :]
    mt, tt, wt = stat[:, 2:3, :], stat[:, 3:4, :], stat[:, 4:5, :]
    top_s, top_t = jnp.max(ms, axis=0), jnp.max(mt, axis=0)
    total_s = jnp.sum(ss * jnp.exp(ms - top_s[None]), axis=0)
    scale_t = jnp.exp(mt - top_t[None])
    total_t = jnp.sum(tt * scale_t, axis=0)
    cross = jnp.sum(wt * scale_t, axis=0) / total_t
    lse_s = top_s + jnp.log(total_s)
    lse_t = top_t + jnp.log(total_t)
    mm_ref[...] = sharpness_divisor * sharpness_divisor * (cross + lse_s - lse_t)
    own = stat[me]
    gain = objective_factor * sharpness_divisor
    rowsbuf[...] = jnp.zeros_like(rowsbuf)
    rowsbuf[0:1, :] = gain * jnp.exp(own[0:1, :] - lse_s)
    rowsbuf[1:2, :] = gain * jnp.exp(own[2:3, :] - lse_t)
    cols[...] = jnp.transpose(rowsbuf[...])

    def derive(b, c):
        rows = pl.ds(pl.multiple_of(b * block, block), block)
        f = cols[rows, :]
        score[rows, :] = (es[rows, :] * f[:, 0:1] - et[rows, :] * f[:, 1:2]).astype(bf16)
        return c
    lax.fori_loop(0, nblk, derive, 0)
    ps = partner(score.at[pl.ds(0, tok)], score.at[pl.ds(tok, tok)], 1)
    ps.start()

    order = [planes[3], planes[2], planes[1], planes[0]]

    def block_of(dy, dx):
        slot = dev(0, dy, dx)
        return pl.ds(pl.multiple_of(slot * width, width), width)

    near, beside, across, diag = block_of(0, 0), block_of(1, 0), block_of(0, 1), block_of(1, 1)
    top, bottom = pl.ds(0, half), pl.ds(half, half)

    def bcopy(k, d, h):
        return remote(sb.at[k, d, h], rb.at[k, d, h], b_send.at[k, d, h],
                      b_recv.at[k, d, h], xdev if d else ydev)

    for k in range(4):
        pp[k] = lax.dot_general(score[:tok, :], w[wrows(order[k] * 4, 4), :], NT,
                                preferred_element_type=f32)
        sa[k, 0] = pp[k, top, diag].astype(bf16)
        sa[k, 1] = pp[k, bottom, diag].astype(bf16)
        go(remote(sa.at[k, 0], ra.at[k, 0], a_send.at[k, 0], a_recv.at[k, 0], xdev))
        go(remote(sa.at[k, 1], ra.at[k, 1], a_send.at[k, 1], a_recv.at[k, 1], ydev))
        sb[k, 0, 1] = pp[k, bottom, beside].astype(bf16)
        go(bcopy(k, 0, 1))
        sb[k, 1, 0] = pp[k, top, across].astype(bf16)
        go(bcopy(k, 1, 0))

    pair = 2

    def weight_part(j, c):
        slot = core * mine + j * pair
        a = jnp.concatenate(
            [jnp.concatenate([gath[slot + i], pgath[j * pair + i]], axis=0) for i in range(pair)],
            axis=1)
        for v in range(2):
            vs = pl.ds(v * (w.shape[1] // 2), w.shape[1] // 2)
            g = lax.dot_general(a, score[:, vs], TN, preferred_element_type=f32)
            wg_ref[pl.ds(pl.multiple_of(j * pair * width, width), pair * width), vs] = g.astype(bf16)
        return c

    def join(k):
        a = remote(sa.at[k, 0], ra.at[k, 0], a_send.at[k, 0], a_recv.at[k, 0], xdev)
        a.wait_recv()
        sb[k, 0, 0] = (pp[k, top, beside] + ra[k, 0].astype(f32)).astype(bf16)
        go(bcopy(k, 0, 0))
        a = remote(sa.at[k, 1], ra.at[k, 1], a_send.at[k, 1], a_recv.at[k, 1], ydev)
        a.wait_recv()
        sb[k, 1, 1] = (pp[k, bottom, across] + ra[k, 1].astype(f32)).astype(bf16)
        go(bcopy(k, 1, 1))

    join(0)
    join(1)
    ph.wait()
    ps.wait()
    lax.fori_loop(0, mine // (2 * pair), weight_part, 0)
    join(2)
    join(3)
    lax.fori_loop(mine // (2 * pair), mine // pair, weight_part, 0)

    for k in range(4):
        for d in range(2):
            for h in range(2):
                bcopy(k, d, h).wait_recv()
        for h in range(2):
            hs = bottom if h else top
            pp[k, hs, near] += rb[k, 0, h].astype(f32) + rb[k, 1, h].astype(f32)
        if k < 3:
            sd[k] = pp[k, :, near].astype(bf16)
            go(remote(sd.at[k], rd.at[z], d_send.at[k], d_recv.at[z], dev(order[k], 0, 0)))
    total = pp[3, :, near]
    for k in range(3):
        zz = order[k]
        remote(sd.at[k], rd.at[zz], d_send.at[k], d_recv.at[zz], dev(zz, 0, 0)).wait_recv()
        total += rd[zz].astype(f32)
    hg_ref[...] = total.astype(bf16)

    for c in pending:
        c.wait_send()

    @pl.when(mid)
    def _():
        for c in pending_mid:
            c.wait_send()

    def stat_done(i, c):
        stat_copy(i).wait_send()
        return c
    lax.fori_loop(1, n, stat_done, 0)

def fused(n, hidden, head_weight, mentor_outputs):
    tok, width = hidden.shape
    feats, voc = head_weight.shape
    half, mine = tok // 2, n // 2
    vm = pltpu.VMEM
    dma = pltpu.SemaphoreType.DMA
    anyspace = pl.BlockSpec(memory_space=pl.ANY)
    vspace = pl.BlockSpec(memory_space=pltpu.VMEM)
    hg, wg, mm = pl.pallas_call(
        stages,
        out_shape=(
            jax.ShapeDtypeStruct((tok, width), bf16),
            jax.ShapeDtypeStruct((feats // 2, voc), bf16),
            jax.ShapeDtypeStruct((1, tok), f32),
        ),
        in_specs=[vspace, anyspace, vspace],
        out_specs=(vspace,) * 3,
        scratch_shapes=[
            vm((n, tok, width), bf16),
            vm((mine, tok, width), bf16),
            vm((feats, voc), bf16),
            vm((tok, voc), f32),
            vm((tok, voc), f32),
            vm((2 * tok, voc), bf16),
            vm((tok, 128), f32),
            vm((128, tok), f32),
            vm((n, 8, tok), f32),
            vm((4, 2, half, width), bf16),
            vm((4, 2, half, width), bf16),
            vm((4, 2, 2, half, width), bf16),
            vm((4, 2, 2, half, width), bf16),
            vm((4, tok, 4 * width), f32),
            vm((3, tok, width), bf16),
            vm((4, tok, width), bf16),
            dma((1,)),
            dma((n, 2)),
            dma((5, 2)),
            dma((4, 4)),
            dma((4, 2)),
            dma((n,)),
            dma((n,)),
            dma((4, 2)),
            dma((4, 2)),
            dma((4, 2, 2)),
            dma((4, 2, 2)),
            dma((3,)),
            dma((4,)),
            dma((2,)),
            dma((2,)),
        ],
        compiler_params=pltpu.CompilerParams(
            collective_id=0, has_side_effects=True, vmem_limit_bytes=48 * 1024 * 1024),
        cost_estimate=pl.CostEstimate(
            flops=6 * tok * feats * voc, transcendentals=2 * tok * voc,
            bytes_accessed=2 * feats * voc + feats * voc),
    )(hidden, head_weight, mentor_outputs)
    return hg, wg, mm.reshape(tok)


def collective(hidden, head_weight, mentor_outputs):
    full_hidden = lax.all_gather(hidden, "vocab", axis=1, tiled=True)
    student = jnp.dot(full_hidden, head_weight, preferred_element_type=f32) / sharpness_divisor
    target = mentor_outputs.astype(f32) / sharpness_divisor
    top_s, top_t = lax.pmax((jnp.max(student, axis=1), jnp.max(target, axis=1)), "vocab")
    exp_s = jnp.exp(student - top_s[:, None])
    exp_t = jnp.exp(target - top_t[:, None])
    total_s, total_t, weighted = lax.psum(
        (jnp.sum(exp_s, axis=1), jnp.sum(exp_t, axis=1),
         jnp.sum(exp_t * (target - student), axis=1)), "vocab")
    lse_s = top_s + jnp.log(total_s)
    lse_t = top_t + jnp.log(total_t)
    mismatch = sharpness_divisor * sharpness_divisor * (weighted / total_t + lse_s - lse_t)
    score = (objective_factor * sharpness_divisor
             * (jnp.exp(student - lse_s[:, None]) - jnp.exp(target - lse_t[:, None]))).astype(bf16)
    hidden_part = lax.psum_scatter(
        lax.dot_general(head_weight, score, NT, preferred_element_type=f32),
        "vocab", scatter_dimension=0, tiled=True)
    weight_grad = lax.psum_scatter(
        lax.dot_general(full_hidden, score, TN, preferred_element_type=f32),
        "rows", scatter_dimension=0, tiled=True).astype(bf16)
    return hidden_part.T.astype(bf16), weight_grad, mismatch


def solution(mesh):
    n = mesh.shape["vocab"]

    def shards(hidden, head_weight, mentor_outputs):
        if n == 16 and mesh.shape["rows"] == 2 and hidden.shape[1] % 128 == 0:
            return fused(n, hidden, head_weight, mentor_outputs)
        return collective(hidden, head_weight, mentor_outputs)

    return jax.shard_map(
        shards,
        mesh=mesh,
        in_specs=(P("rows", "vocab"), P(None, "vocab"), P("rows", "vocab")),
        out_specs=(P("rows", "vocab"), P("rows", "vocab"), P("rows")),
        check_vma=False,
    )
```

```python
import functools

import jax
import jax.numpy as jnp
from jax import lax
from jax.experimental import pallas as pl
from jax.experimental.pallas import tpu as pltpu
from jax.sharding import PartitionSpec as P

sharpness_divisor = 2.0
objective_factor = 32.0
f32 = jnp.float32
bf16 = jnp.bfloat16

NT = (((1,), (1,)), ((), ()))
TN = (((0,), (0,)), ((), ()))


def stages(h_ref, w_hbm, t, hg_ref, wg_ref, mm_ref,
           gath, pgath, w, es, et, score, cols, rowsbuf, stat,
           sx, rx, sy, ry, sj, rj, pp, sd, rd,
           loc_sem, ag_recv, z_send, xy_send, f_send, st_send, st_recv,
           x_send, x_recv, y_send, y_recv, j_send, j_recv, d_send, d_recv, p_send, p_recv):
    n = gath.shape[0]
    tok, width = h_ref.shape
    half = tok // 2
    me = lax.axis_index("vocab")
    core = lax.axis_index("rows")
    z, y, x = me // 4, lax.rem(me // 2, 2), lax.rem(me, 2)
    mid = jnp.logical_or(z == 1, z == 2)

    def dev(zz, dy, dx):
        yy = 1 - y if dy else y
        xx = 1 - x if dx else x
        return zz * 4 + yy * 2 + xx

    z_near = z + 1 - 2 * lax.rem(z, 2)
    z_in = 3 - z
    low = z // 2
    planes = [z, z_near, 2 - low, 3 - 3 * low]
    xdev, ydev = dev(z, 0, 1), dev(z, 1, 0)

    def remote(src, dst, ss, rs, target):
        return pltpu.make_async_remote_copy(
            src_ref=src, dst_ref=dst, send_sem=ss, recv_sem=rs,
            device_id={"vocab": target}, device_id_type=pl.DeviceIdType.MESH)

    def partner(src, dst, i):
        return pltpu.make_async_remote_copy(
            src_ref=src, dst_ref=dst, send_sem=p_send.at[i], recv_sem=p_recv.at[i],
            device_id={"rows": 1 - core}, device_id_type=pl.DeviceIdType.MESH)

    cp_w = pltpu.make_async_copy(w_hbm, w, loc_sem.at[0])
    cp_w.start()
    gath[me] = h_ref[...]

    barrier = pltpu.get_barrier_semaphore()

    def greet(i, c):
        pl.semaphore_signal(barrier, inc=1, device_id={"vocab": lax.rem(me + i, n)},
                            device_id_type=pl.DeviceIdType.MESH)
        return c
    lax.fori_loop(1, n, greet, 0)
    pl.semaphore_signal(barrier, inc=1, device_id={"rows": 1 - core},
                        device_id_type=pl.DeviceIdType.MESH)
    pl.semaphore_wait(barrier, n)

    def gcopy(slot, h, ss, target):
        ref = gath.at[slot] if h is None else gath.at[slot, pl.ds(h * half, half)]
        return remote(ref, ref, ss, ag_recv.at[slot, h or 0], target)

    def wait_piece(slot, h=None):
        gcopy(slot, h, f_send.at[0, 0], xdev).wait_recv()

    pending, pending_mid = [], []

    def go(c):
        c.start()
        pending.append(c)

    def go_mid(c):
        pl.when(mid)(c.start)
        pending_mid.append(c)

    def fan_out(i):
        slot = dev(planes[i], 0, 0)
        go(gcopy(slot, None, xy_send.at[i, 0], ydev))
        go(gcopy(slot, None, xy_send.at[i, 1], xdev))

    def forward(i):
        s0, s1 = dev(planes[i], 1, 0), dev(planes[i], 0, 1)
        wait_piece(s0)
        go(gcopy(s0, 0, f_send.at[i, 0], xdev))
        wait_piece(s1)
        go(gcopy(s1, 1, f_send.at[i, 1], ydev))

    def wrows(slot, count):
        return pl.ds(pl.multiple_of(slot * width, width), count * width)

    def multiply(slot, count, first=False):
        a = jnp.concatenate([gath[slot + c] for c in range(count)], axis=1)
        part = jnp.dot(a, w[wrows(slot, count), :], preferred_element_type=f32)
        if first:
            es[...] = part
        else:
            es[...] += part

    def plane(i):
        s = dev(planes[i], 1, 1)
        if i == 3:
            multiply(planes[3] * 4 + 2 * y, 2)
        wait_piece(s, 0)
        wait_piece(s, 1)
        if i == 3:
            multiply(planes[3] * 4 + 2 * (1 - y), 2)
        else:
            multiply(planes[i] * 4, 4, i == 0)

    zn_dev, zi_dev = dev(z_near, 0, 0), dev(z_in, 0, 0)
    go(gcopy(me, None, z_send.at[0], zn_dev))
    go_mid(gcopy(me, None, z_send.at[1], zi_dev))
    fan_out(0)

    block = 32
    nblk = tok // block
    lane = lax.broadcasted_iota(jnp.int32, (block, 128), 1)

    def teacher(b, c):
        rows = pl.ds(pl.multiple_of(b * block, block), block)
        tv = t[rows, :].astype(f32) / sharpness_divisor
        m = jnp.max(tv, axis=1, keepdims=True)
        e = jnp.exp(tv - m)
        et[rows, :] = e
        total = jnp.sum(e, axis=1, keepdims=True)
        cols[rows, :] = jnp.where(lane == 2, m, jnp.where(lane == 3, total, 0.0))
        return c
    lax.fori_loop(0, nblk, teacher, 0)

    for i in range(1, 4):
        slot = dev(planes[i], 0, 0)
        target = zi_dev if i == 1 else zn_dev
        wait_piece(slot)
        go_mid(gcopy(slot, None, z_send.at[1 + i], target))
        fan_out(i)
        forward(i - 1)
        if i > 1:
            if i == 2:
                cp_w.wait()
            plane(i - 2)
    forward(3)
    plane(2)
    plane(3)

    mine = n // 2
    ph = partner(gath.at[pl.ds((1 - core) * mine, mine)], pgath, 0)
    ph.start()

    def student(b, c):
        rows = pl.ds(pl.multiple_of(b * block, block), block)
        sv = es[rows, :] / sharpness_divisor
        tv = t[rows, :].astype(f32) / sharpness_divisor
        m = jnp.max(sv, axis=1, keepdims=True)
        e = jnp.exp(sv - m)
        es[rows, :] = e
        total = jnp.sum(e, axis=1, keepdims=True)
        weighted = jnp.sum(et[rows, :] * (tv - sv), axis=1, keepdims=True)
        old = cols[rows, :]
        cols[rows, :] = jnp.where(
            lane == 0, m, jnp.where(lane == 1, total, jnp.where(lane == 4, weighted, old)))
        return c
    lax.fori_loop(0, nblk, student, 0)
    stat[me] = jnp.transpose(cols[...])[:8, :]

    def stat_copy(i):
        return remote(stat.at[me], stat.at[me], st_send.at[i], st_recv.at[me],
                      lax.rem(me + i, n))

    def stat_start(i, c):
        stat_copy(i).start()
        return c
    lax.fori_loop(1, n, stat_start, 0)

    def stat_wait(i, c):
        other = lax.rem(me + i, n)
        remote(stat.at[other], stat.at[other], st_send.at[i], st_recv.at[other],
               other).wait_recv()
        return c
    lax.fori_loop(1, n, stat_wait, 0)

    ms, ss = stat[:, 0:1, :], stat[:, 1:2, :]
    mt, tt, wt = stat[:, 2:3, :], stat[:, 3:4, :], stat[:, 4:5, :]
    top_s, top_t = jnp.max(ms, axis=0), jnp.max(mt, axis=0)
    total_s = jnp.sum(ss * jnp.exp(ms - top_s[None]), axis=0)
    scale_t = jnp.exp(mt - top_t[None])
    total_t = jnp.sum(tt * scale_t, axis=0)
    cross = jnp.sum(wt * scale_t, axis=0) / total_t
    lse_s = top_s + jnp.log(total_s)
    lse_t = top_t + jnp.log(total_t)
    mm_ref[...] = sharpness_divisor * sharpness_divisor * (cross + lse_s - lse_t)
    own = stat[me]
    gain = objective_factor * sharpness_divisor
    rowsbuf[...] = jnp.zeros_like(rowsbuf)
    rowsbuf[0:1, :] = gain * jnp.exp(own[0:1, :] - lse_s)
    rowsbuf[1:2, :] = gain * jnp.exp(own[2:3, :] - lse_t)
    cols[...] = jnp.transpose(rowsbuf[...])

    def derive(b, c):
        rows = pl.ds(pl.multiple_of(b * block, block), block)
        f = cols[rows, :]
        score[rows, :] = (es[rows, :] * f[:, 0:1] - et[rows, :] * f[:, 1:2]).astype(bf16)
        return c
    lax.fori_loop(0, nblk, derive, 0)
    ps = partner(score.at[pl.ds(0, tok)], score.at[pl.ds(tok, tok)], 1)
    ps.start()

    order = [planes[3], planes[2], planes[1], planes[0]]

    def block_of(dy, dx):
        slot = dev(0, dy, dx)
        return pl.ds(pl.multiple_of(slot * width, width), width)

    near, beside, across, diag = block_of(0, 0), block_of(1, 0), block_of(0, 1), block_of(1, 1)
    top, bottom = pl.ds(0, half), pl.ds(half, half)

    def xcopy(k):
        return remote(sx.at[k], rx.at[k], x_send.at[k], x_recv.at[k], xdev)

    def ycopy(k):
        return remote(sy.at[k], ry.at[k], y_send.at[k], y_recv.at[k], ydev)

    def jcopy(k, d):
        return remote(sj.at[k, d], rj.at[k, d], j_send.at[k, d], j_recv.at[k, d],
                      xdev if d else ydev)

    for k in range(4):
        pp[k] = lax.dot_general(score[:tok, :], w[wrows(order[k] * 4, 4), :], NT,
                                preferred_element_type=f32)
        sx[k, 0] = pp[k, top, diag].astype(bf16)
        sx[k, 1] = pp[k, top, across].astype(bf16)
        go(xcopy(k))
        sy[k, 0] = pp[k, bottom, diag].astype(bf16)
        sy[k, 1] = pp[k, bottom, beside].astype(bf16)
        go(ycopy(k))

    pair = 2

    def weight_part(j, c):
        slot = core * mine + j * pair
        a = jnp.concatenate(
            [jnp.concatenate([gath[slot + i], pgath[j * pair + i]], axis=0) for i in range(pair)],
            axis=1)
        for v in range(2):
            vs = pl.ds(v * (w.shape[1] // 2), w.shape[1] // 2)
            g = lax.dot_general(a, score[:, vs], TN, preferred_element_type=f32)
            wg_ref[pl.ds(pl.multiple_of(j * pair * width, width), pair * width), vs] = g.astype(bf16)
        return c

    def join(k):
        xcopy(k).wait_recv()
        sj[k, 0] = (pp[k, top, beside] + rx[k, 0].astype(f32)).astype(bf16)
        go(jcopy(k, 0))
        ycopy(k).wait_recv()
        sj[k, 1] = (pp[k, bottom, across] + ry[k, 0].astype(f32)).astype(bf16)
        go(jcopy(k, 1))

    def column(k):
        jcopy(k, 0).wait_recv()
        pp[k, top, near] += rj[k, 0].astype(f32) + rx[k, 1].astype(f32)
        jcopy(k, 1).wait_recv()
        pp[k, bottom, near] += rj[k, 1].astype(f32) + ry[k, 1].astype(f32)
        if k < 3:
            sd[k] = pp[k, :, near].astype(bf16)
            go(remote(sd.at[k], rd.at[z], d_send.at[k], d_recv.at[z], dev(order[k], 0, 0)))

    chunks = mine // pair

    def wait_partner():
        ph.wait()
        ps.wait()

    join(0)
    join(1)
    pl.when(core == 0)(wait_partner)
    lax.fori_loop(0, (1 - core) * (chunks // 2), weight_part, 0)
    join(2)
    join(3)
    column(0)
    lax.fori_loop((1 - core) * (chunks // 2), (1 - core) * chunks, weight_part, 0)
    column(1)
    column(2)
    pl.when(core == 1)(wait_partner)
    lax.fori_loop(0, core * chunks, weight_part, 0)
    column(3)
    total = pp[3, :, near]
    for k in range(3):
        zz = order[k]
        remote(sd.at[k], rd.at[zz], d_send.at[k], d_recv.at[zz], dev(zz, 0, 0)).wait_recv()
        total += rd[zz].astype(f32)
    hg_ref[...] = total.astype(bf16)

    for c in pending:
        c.wait_send()

    @pl.when(mid)
    def _():
        for c in pending_mid:
            c.wait_send()

    def stat_done(i, c):
        stat_copy(i).wait_send()
        return c
    lax.fori_loop(1, n, stat_done, 0)

def fused(n, hidden, head_weight, mentor_outputs):
    tok, width = hidden.shape
    feats, voc = head_weight.shape
    half, mine = tok // 2, n // 2
    vm = pltpu.VMEM
    dma = pltpu.SemaphoreType.DMA
    anyspace = pl.BlockSpec(memory_space=pl.ANY)
    vspace = pl.BlockSpec(memory_space=pltpu.VMEM)
    hg, wg, mm = pl.pallas_call(
        stages,
        out_shape=(
            jax.ShapeDtypeStruct((tok, width), bf16),
            jax.ShapeDtypeStruct((feats // 2, voc), bf16),
            jax.ShapeDtypeStruct((1, tok), f32),
        ),
        in_specs=[vspace, anyspace, vspace],
        out_specs=(vspace,) * 3,
        scratch_shapes=[
            vm((n, tok, width), bf16),
            vm((mine, tok, width), bf16),
            vm((feats, voc), bf16),
            vm((tok, voc), f32),
            vm((tok, voc), f32),
            vm((2 * tok, voc), bf16),
            vm((tok, 128), f32),
            vm((128, tok), f32),
            vm((n, 8, tok), f32),
            vm((4, 2, half, width), bf16),
            vm((4, 2, half, width), bf16),
            vm((4, 2, half, width), bf16),
            vm((4, 2, half, width), bf16),
            vm((4, 2, half, width), bf16),
            vm((4, 2, half, width), bf16),
            vm((4, tok, 4 * width), f32),
            vm((3, tok, width), bf16),
            vm((4, tok, width), bf16),
            dma((1,)),
            dma((n, 2)),
            dma((5,)),
            dma((4, 2)),
            dma((4, 2)),
            dma((n,)),
            dma((n,)),
            dma((4,)),
            dma((4,)),
            dma((4,)),
            dma((4,)),
            dma((4, 2)),
            dma((4, 2)),
            dma((3,)),
            dma((4,)),
            dma((2,)),
            dma((2,)),
        ],
        compiler_params=pltpu.CompilerParams(
            collective_id=0, has_side_effects=True, vmem_limit_bytes=48 * 1024 * 1024),
        cost_estimate=pl.CostEstimate(
            flops=6 * tok * feats * voc, transcendentals=2 * tok * voc,
            bytes_accessed=2 * feats * voc + feats * voc),
    )(hidden, head_weight, mentor_outputs)
    return hg, wg, mm.reshape(tok)


def collective(hidden, head_weight, mentor_outputs):
    full_hidden = lax.all_gather(hidden, "vocab", axis=1, tiled=True)
    student = jnp.dot(full_hidden, head_weight, preferred_element_type=f32) / sharpness_divisor
    target = mentor_outputs.astype(f32) / sharpness_divisor
    top_s, top_t = lax.pmax((jnp.max(student, axis=1), jnp.max(target, axis=1)), "vocab")
    exp_s = jnp.exp(student - top_s[:, None])
    exp_t = jnp.exp(target - top_t[:, None])
    total_s, total_t, weighted = lax.psum(
        (jnp.sum(exp_s, axis=1), jnp.sum(exp_t, axis=1),
         jnp.sum(exp_t * (target - student), axis=1)), "vocab")
    lse_s = top_s + jnp.log(total_s)
    lse_t = top_t + jnp.log(total_t)
    mismatch = sharpness_divisor * sharpness_divisor * (weighted / total_t + lse_s - lse_t)
    score = (objective_factor * sharpness_divisor
             * (jnp.exp(student - lse_s[:, None]) - jnp.exp(target - lse_t[:, None]))).astype(bf16)
    hidden_part = lax.psum_scatter(
        lax.dot_general(head_weight, score, NT, preferred_element_type=f32),
        "vocab", scatter_dimension=0, tiled=True)
    weight_grad = lax.psum_scatter(
        lax.dot_general(full_hidden, score, TN, preferred_element_type=f32),
        "rows", scatter_dimension=0, tiled=True).astype(bf16)
    return hidden_part.T.astype(bf16), weight_grad, mismatch


def solution(mesh):
    n = mesh.shape["vocab"]

    def shards(hidden, head_weight, mentor_outputs):
        if n == 16 and mesh.shape["rows"] == 2 and hidden.shape[1] % 128 == 0:
            return fused(n, hidden, head_weight, mentor_outputs)
        return collective(hidden, head_weight, mentor_outputs)

    return jax.shard_map(
        shards,
        mesh=mesh,
        in_specs=(P("rows", "vocab"), P(None, "vocab"), P("rows", "vocab")),
        out_specs=(P("rows", "vocab"), P("rows", "vocab"), P("rows")),
        check_vma=False,
    )
```

```python
import functools

import jax
import jax.numpy as jnp
from jax import lax
from jax.experimental import pallas as pl
from jax.experimental.pallas import tpu as pltpu
from jax.sharding import PartitionSpec as P

sharpness_divisor = 2.0
objective_factor = 32.0
f32 = jnp.float32
bf16 = jnp.bfloat16

NT = (((1,), (1,)), ((), ()))
TN = (((0,), (0,)), ((), ()))
BATCHES = 2


def stages(h_ref, w_hbm, t, hg_ref, wg_ref, mm_ref,
           gath, pgath, w, es, et, score, cols, rowsbuf, stat,
           sx, rx, sy, ry, sj, rj, pp, sd, rd,
           loc_sem, ag_recv, z_send, xy_send, f_send, st_send, st_recv,
           x_send, x_recv, y_send, y_recv, j_send, j_recv, d_send, d_recv, p_send, p_recv):
    n = gath.shape[0]
    tok, width = h_ref.shape
    batch = tok // BATCHES
    half = batch // 2
    me = lax.axis_index("vocab")
    core = lax.axis_index("rows")
    z, y, x = me // 4, lax.rem(me // 2, 2), lax.rem(me, 2)
    mid = jnp.logical_or(z == 1, z == 2)

    def dev(zz, dy, dx):
        yy = 1 - y if dy else y
        xx = 1 - x if dx else x
        return zz * 4 + yy * 2 + xx

    z_near = z + 1 - 2 * lax.rem(z, 2)
    z_in = 3 - z
    low = z // 2
    planes = [z, z_near, 2 - low, 3 - 3 * low]
    order = planes[::-1]
    xdev, ydev = dev(z, 0, 1), dev(z, 1, 0)
    zn_dev, zi_dev = dev(z_near, 0, 0), dev(z_in, 0, 0)

    def remote(src, dst, ss, rs, target):
        return pltpu.make_async_remote_copy(
            src_ref=src, dst_ref=dst, send_sem=ss, recv_sem=rs,
            device_id={"vocab": target}, device_id_type=pl.DeviceIdType.MESH)

    def partner(src, dst, i):
        return pltpu.make_async_remote_copy(
            src_ref=src, dst_ref=dst, send_sem=p_send.at[i], recv_sem=p_recv.at[i],
            device_id={"rows": 1 - core}, device_id_type=pl.DeviceIdType.MESH)

    cp_w = pltpu.make_async_copy(w_hbm, w, loc_sem.at[0])
    cp_w.start()
    gath[me] = h_ref[...]

    barrier = pltpu.get_barrier_semaphore()

    def greet(i, c):
        pl.semaphore_signal(barrier, inc=1, device_id={"vocab": lax.rem(me + i, n)},
                            device_id_type=pl.DeviceIdType.MESH)
        return c
    lax.fori_loop(1, n, greet, 0)
    pl.semaphore_signal(barrier, inc=1, device_id={"rows": 1 - core},
                        device_id_type=pl.DeviceIdType.MESH)
    pl.semaphore_wait(barrier, n)

    pending, pending_mid = [], []

    def go(c):
        c.start()
        pending.append(c)

    def go_mid(c):
        pl.when(mid)(c.start)
        pending_mid.append(c)

    def gcopy(b, slot, h, ss, target):
        start, size = (b * batch, batch) if h is None else (b * batch + h * half, half)
        ref = gath.at[slot, pl.ds(start, size)]
        return remote(ref, ref, ss, ag_recv.at[slot, b, h or 0], target)

    def wait_piece(b, slot, h=None):
        gcopy(b, slot, h, f_send.at[b, 0, 0], xdev).wait_recv()

    def z_start(b):
        go(gcopy(b, me, None, z_send.at[b, 0], zn_dev))
        go_mid(gcopy(b, me, None, z_send.at[b, 1], zi_dev))

    def z_step(b, i):
        slot = dev(planes[i], 0, 0)
        wait_piece(b, slot)
        go_mid(gcopy(b, slot, None, z_send.at[b, 1 + i], zi_dev if i == 1 else zn_dev))

    def fan_out(b, i):
        slot = dev(planes[i], 0, 0)
        go(gcopy(b, slot, None, xy_send.at[b, i, 0], ydev))
        go(gcopy(b, slot, None, xy_send.at[b, i, 1], xdev))

    def forward(b, i):
        s0, s1 = dev(planes[i], 1, 0), dev(planes[i], 0, 1)
        wait_piece(b, s0)
        go(gcopy(b, s0, 0, f_send.at[b, i, 0], xdev))
        wait_piece(b, s1)
        go(gcopy(b, s1, 1, f_send.at[b, i, 1], ydev))

    def wrows(slot, count):
        return pl.ds(pl.multiple_of(slot * width, width), count * width)

    def brows(b):
        return pl.ds(b * batch, batch)

    def multiply(b, slot, count, first=False):
        a = jnp.concatenate([gath[slot + c, brows(b), :] for c in range(count)], axis=1)
        part = jnp.dot(a, w[wrows(slot, count), :], preferred_element_type=f32)
        if first:
            es[brows(b), :] = part
        else:
            es[brows(b), :] += part

    def plane(b, i):
        s = dev(planes[i], 1, 1)
        if i == 3:
            multiply(b, planes[3] * 4 + 2 * y, 2)
        wait_piece(b, s, 0)
        wait_piece(b, s, 1)
        if i == 3:
            multiply(b, planes[3] * 4 + 2 * (1 - y), 2)
        else:
            multiply(b, planes[i] * 4, 4, i == 0)

    block = 32
    nblk = batch // block
    lane = lax.broadcasted_iota(jnp.int32, (block, 128), 1)

    def teacher(i, c):
        rows = pl.ds(pl.multiple_of(i * block, block), block)
        tv = t[rows, :].astype(f32) / sharpness_divisor
        m = jnp.max(tv, axis=1, keepdims=True)
        e = jnp.exp(tv - m)
        et[rows, :] = e
        total = jnp.sum(e, axis=1, keepdims=True)
        cols[rows, :] = jnp.where(lane == 2, m, jnp.where(lane == 3, total, 0.0))
        return c

    def student(i, c):
        rows = pl.ds(pl.multiple_of(i * block, block), block)
        sv = es[rows, :] / sharpness_divisor
        tv = t[rows, :].astype(f32) / sharpness_divisor
        m = jnp.max(sv, axis=1, keepdims=True)
        e = jnp.exp(sv - m)
        es[rows, :] = e
        total = jnp.sum(e, axis=1, keepdims=True)
        weighted = jnp.sum(et[rows, :] * (tv - sv), axis=1, keepdims=True)
        old = cols[rows, :]
        cols[rows, :] = jnp.where(
            lane == 0, m, jnp.where(lane == 1, total, jnp.where(lane == 4, weighted, old)))
        return c

    def stat_copy(b, i):
        return remote(stat.at[b, me], stat.at[b, me], st_send.at[b, i], st_recv.at[b, me],
                      lax.rem(me + i, n))

    def stat_send(b):
        lax.fori_loop(b * nblk, (b + 1) * nblk, student, 0)
        stat[b, me] = jnp.transpose(cols[brows(b), :])[:8, :]

        def start(i, c):
            stat_copy(b, i).start()
            return c
        lax.fori_loop(1, n, start, 0)

    def derive(i, c):
        rows = pl.ds(pl.multiple_of(i * block, block), block)
        f = cols[rows, :]
        score[rows, :] = (es[rows, :] * f[:, 0:1] - et[rows, :] * f[:, 1:2]).astype(bf16)
        return c

    def stat_join(b):
        def wait(i, c):
            other = lax.rem(me + i, n)
            remote(stat.at[b, other], stat.at[b, other], st_send.at[b, i],
                   st_recv.at[b, other], other).wait_recv()
            return c
        lax.fori_loop(1, n, wait, 0)
        ms, ss = stat[b, :, 0:1, :], stat[b, :, 1:2, :]
        mt, tt, wt = stat[b, :, 2:3, :], stat[b, :, 3:4, :], stat[b, :, 4:5, :]
        top_s, top_t = jnp.max(ms, axis=0), jnp.max(mt, axis=0)
        total_s = jnp.sum(ss * jnp.exp(ms - top_s[None]), axis=0)
        scale_t = jnp.exp(mt - top_t[None])
        total_t = jnp.sum(tt * scale_t, axis=0)
        cross = jnp.sum(wt * scale_t, axis=0) / total_t
        lse_s = top_s + jnp.log(total_s)
        lse_t = top_t + jnp.log(total_t)
        mm_ref[:, brows(b)] = sharpness_divisor * sharpness_divisor * (cross + lse_s - lse_t)
        own = stat[b, me]
        gain = objective_factor * sharpness_divisor
        rowsbuf[b, 0:1, :] = gain * jnp.exp(own[0:1, :] - lse_s)
        rowsbuf[b, 1:2, :] = gain * jnp.exp(own[2:3, :] - lse_t)
        cols[brows(b), :] = jnp.transpose(rowsbuf[b])
        lax.fori_loop(b * nblk, (b + 1) * nblk, derive, 0)

    def block_of(dy, dx):
        return pl.ds(pl.multiple_of(dev(0, dy, dx) * width, width), width)

    near, beside, across, diag = block_of(0, 0), block_of(1, 0), block_of(0, 1), block_of(1, 1)
    top, bottom = pl.ds(0, half), pl.ds(half, half)

    def xcopy(b, k):
        return remote(sx.at[b, k], rx.at[b, k], x_send.at[b, k], x_recv.at[b, k], xdev)

    def ycopy(b, k):
        return remote(sy.at[b, k], ry.at[b, k], y_send.at[b, k], y_recv.at[b, k], ydev)

    def jcopy(b, k, d):
        return remote(sj.at[b, k, d], rj.at[b, k, d], j_send.at[b, k, d], j_recv.at[b, k, d],
                      xdev if d else ydev)

    def spread(b):
        for k in range(4):
            pp[b, k] = lax.dot_general(score[brows(b), :], w[wrows(order[k] * 4, 4), :], NT,
                                       preferred_element_type=f32)
            sx[b, k, 0] = pp[b, k, top, diag].astype(bf16)
            sx[b, k, 1] = pp[b, k, top, across].astype(bf16)
            go(xcopy(b, k))
            sy[b, k, 0] = pp[b, k, bottom, diag].astype(bf16)
            sy[b, k, 1] = pp[b, k, bottom, beside].astype(bf16)
            go(ycopy(b, k))

    def join(b, k):
        xcopy(b, k).wait_recv()
        sj[b, k, 0] = (pp[b, k, top, beside] + rx[b, k, 0].astype(f32)).astype(bf16)
        go(jcopy(b, k, 0))
        ycopy(b, k).wait_recv()
        sj[b, k, 1] = (pp[b, k, bottom, across] + ry[b, k, 0].astype(f32)).astype(bf16)
        go(jcopy(b, k, 1))

    def column(b, k):
        jcopy(b, k, 0).wait_recv()
        pp[b, k, top, near] += rj[b, k, 0].astype(f32) + rx[b, k, 1].astype(f32)
        jcopy(b, k, 1).wait_recv()
        pp[b, k, bottom, near] += rj[b, k, 1].astype(f32) + ry[b, k, 1].astype(f32)
        if k < 3:
            sd[b, k] = pp[b, k, :, near].astype(bf16)
            go(remote(sd.at[b, k], rd.at[b, z], d_send.at[b, k], d_recv.at[b, z],
                      dev(order[k], 0, 0)))

    def finish(b):
        total = pp[b, 3, :, near]
        for k in range(3):
            zz = order[k]
            remote(sd.at[b, k], rd.at[b, zz], d_send.at[b, k], d_recv.at[b, zz],
                   dev(zz, 0, 0)).wait_recv()
            total += rd[b, zz].astype(f32)
        hg_ref[brows(b), :] = total.astype(bf16)

    mine = n // 2

    pair = 2
    chunks = mine // pair

    def weight_part(j, c):
        slot = core * mine + j * pair
        a = jnp.concatenate(
            [jnp.concatenate([gath[slot + i], pgath[j * pair + i]], axis=0) for i in range(pair)],
            axis=1)
        for v in range(2):
            vs = pl.ds(v * (w.shape[1] // 2), w.shape[1] // 2)
            g = lax.dot_general(a, score[:, vs], TN, preferred_element_type=f32)
            wg_ref[pl.ds(pl.multiple_of(j * pair * width, width), pair * width), vs] = g.astype(bf16)
        return c

    z_start(0)
    fan_out(0, 0)
    z_start(1)
    rowsbuf[...] = jnp.zeros_like(rowsbuf)
    lax.fori_loop(0, BATCHES * nblk, teacher, 0)
    for i in range(1, 4):
        z_step(0, i)
        fan_out(0, i)
        z_step(1, i)
        forward(0, i - 1)
        if i > 1:
            if i == 2:
                cp_w.wait()
            plane(0, i - 2)
    forward(0, 3)
    for i in range(4):
        fan_out(1, i)
    plane(0, 2)
    plane(0, 3)
    stat_send(0)
    forward(1, 0)
    forward(1, 1)
    plane(1, 0)
    forward(1, 2)
    forward(1, 3)
    stat_join(0)
    spread(0)
    for i in range(1, 4):
        plane(1, i)
    ph = partner(gath.at[pl.ds((1 - core) * mine, mine)], pgath, 0)
    ph.start()
    stat_send(1)
    for k in range(4):
        join(0, k)
    stat_join(1)
    ps = partner(score.at[pl.ds(0, tok)], score.at[pl.ds(tok, tok)], 1)
    ps.start()
    spread(1)
    for k in range(4):
        column(0, k)

    def wait_partner():
        ph.wait()
        ps.wait()

    join(1, 0)
    join(1, 1)
    pl.when(core == 0)(wait_partner)
    lax.fori_loop(0, (1 - core) * (chunks // 2), weight_part, 0)
    join(1, 2)
    join(1, 3)
    finish(0)
    column(1, 0)
    lax.fori_loop((1 - core) * (chunks // 2), (1 - core) * chunks, weight_part, 0)
    column(1, 1)
    column(1, 2)
    pl.when(core == 1)(wait_partner)
    lax.fori_loop(0, core * chunks, weight_part, 0)
    column(1, 3)
    finish(1)

    for c in pending:
        c.wait_send()

    @pl.when(mid)
    def _():
        for c in pending_mid:
            c.wait_send()

    def stat_done(i, c):
        for b in range(BATCHES):
            stat_copy(b, i).wait_send()
        return c
    lax.fori_loop(1, n, stat_done, 0)


def fused(n, hidden, head_weight, mentor_outputs):
    tok, width = hidden.shape
    feats, voc = head_weight.shape
    batch, mine = tok // BATCHES, n // 2
    half = batch // 2
    nb = BATCHES
    vm = pltpu.VMEM
    dma = pltpu.SemaphoreType.DMA
    anyspace = pl.BlockSpec(memory_space=pl.ANY)
    vspace = pl.BlockSpec(memory_space=pltpu.VMEM)
    shapes = (
        jax.ShapeDtypeStruct((tok, width), bf16),
        jax.ShapeDtypeStruct((feats // 2, voc), bf16),
        jax.ShapeDtypeStruct((1, tok), f32),
    )
    hg, wg, mm = pl.pallas_call(
        stages,
        out_shape=shapes,
        in_specs=[vspace, anyspace, vspace],
        out_specs=(vspace,) * 3,
        scratch_shapes=[
            vm((n, tok, width), bf16),
            vm((mine, tok, width), bf16),
            vm((feats, voc), bf16),
            vm((tok, voc), f32),
            vm((tok, voc), f32),
            vm((2 * tok, voc), bf16),
            vm((tok, 128), f32),
            vm((nb, 128, batch), f32),
            vm((nb, n, 8, batch), f32),
            vm((nb, 4, 2, half, width), bf16),
            vm((nb, 4, 2, half, width), bf16),
            vm((nb, 4, 2, half, width), bf16),
            vm((nb, 4, 2, half, width), bf16),
            vm((nb, 4, 2, half, width), bf16),
            vm((nb, 4, 2, half, width), bf16),
            vm((nb, 4, batch, 4 * width), f32),
            vm((nb, 3, batch, width), bf16),
            vm((nb, 4, batch, width), bf16),
            dma((1,)),
            dma((n, nb, 2)),
            dma((nb, 5)),
            dma((nb, 4, 2)),
            dma((nb, 4, 2)),
            dma((nb, n)),
            dma((nb, n)),
            dma((nb, 4)),
            dma((nb, 4)),
            dma((nb, 4)),
            dma((nb, 4)),
            dma((nb, 4, 2)),
            dma((nb, 4, 2)),
            dma((nb, 3)),
            dma((nb, 4)),
            dma((2,)),
            dma((2,)),
        ],
        compiler_params=pltpu.CompilerParams(
            collective_id=0, has_side_effects=True, vmem_limit_bytes=48 * 1024 * 1024),
        cost_estimate=pl.CostEstimate(
            flops=6 * tok * feats * voc, transcendentals=2 * tok * voc,
            bytes_accessed=2 * feats * voc + feats * voc),
    )(hidden, head_weight, mentor_outputs)
    return hg, wg, mm.reshape(tok)


def collective(hidden, head_weight, mentor_outputs):
    full_hidden = lax.all_gather(hidden, "vocab", axis=1, tiled=True)
    student = jnp.dot(full_hidden, head_weight, preferred_element_type=f32) / sharpness_divisor
    target = mentor_outputs.astype(f32) / sharpness_divisor
    top_s, top_t = lax.pmax((jnp.max(student, axis=1), jnp.max(target, axis=1)), "vocab")
    exp_s = jnp.exp(student - top_s[:, None])
    exp_t = jnp.exp(target - top_t[:, None])
    total_s, total_t, weighted = lax.psum(
        (jnp.sum(exp_s, axis=1), jnp.sum(exp_t, axis=1),
         jnp.sum(exp_t * (target - student), axis=1)), "vocab")
    lse_s = top_s + jnp.log(total_s)
    lse_t = top_t + jnp.log(total_t)
    mismatch = sharpness_divisor * sharpness_divisor * (weighted / total_t + lse_s - lse_t)
    score = (objective_factor * sharpness_divisor
             * (jnp.exp(student - lse_s[:, None]) - jnp.exp(target - lse_t[:, None]))).astype(bf16)
    hidden_part = lax.psum_scatter(
        lax.dot_general(head_weight, score, NT, preferred_element_type=f32),
        "vocab", scatter_dimension=0, tiled=True)
    weight_grad = lax.psum_scatter(
        lax.dot_general(full_hidden, score, TN, preferred_element_type=f32),
        "rows", scatter_dimension=0, tiled=True).astype(bf16)
    return hidden_part.T.astype(bf16), weight_grad, mismatch


def solution(mesh):
    n = mesh.shape["vocab"]

    def shards(hidden, head_weight, mentor_outputs):
        if n == 16 and mesh.shape["rows"] == 2 and hidden.shape[1] % 128 == 0:
            return fused(n, hidden, head_weight, mentor_outputs)
        return collective(hidden, head_weight, mentor_outputs)

    return jax.shard_map(
        shards,
        mesh=mesh,
        in_specs=(P("rows", "vocab"), P(None, "vocab"), P("rows", "vocab")),
        out_specs=(P("rows", "vocab"), P("rows", "vocab"), P("rows")),
        check_vma=False,
    )
```

```python
import functools

import jax
import jax.numpy as jnp
from jax import lax
from jax.experimental import pallas as pl
from jax.experimental.pallas import tpu as pltpu
from jax.sharding import PartitionSpec as P

sharpness_divisor = 2.0
objective_factor = 32.0
f32 = jnp.float32
bf16 = jnp.bfloat16

NT = (((1,), (1,)), ((), ()))
TN = (((0,), (0,)), ((), ()))


def stages(h_ref, w_hbm, t, hg_ref, wg_ref, mm_ref,
           gath, pgath, w, es, et, score, cols, rowsbuf, stat,
           sx, rx, sy, ry, sj, rj, sn, rn, pp, sd, rd,
           loc_sem, ag_recv, z_send, xy_send, f_send, st_send, st_recv,
           x_send, x_recv, y_send, y_recv, j_send, j_recv, n_send, n_recv, d_send, d_recv, p_send, p_recv):
    n = gath.shape[0]
    tok, width = h_ref.shape
    half = tok // 2
    me = lax.axis_index("vocab")
    core = lax.axis_index("rows")
    z, y, x = me // 4, lax.rem(me // 2, 2), lax.rem(me, 2)
    mid = jnp.logical_or(z == 1, z == 2)

    def dev(zz, dy, dx):
        yy = 1 - y if dy else y
        xx = 1 - x if dx else x
        return zz * 4 + yy * 2 + xx

    z_near = z + 1 - 2 * lax.rem(z, 2)
    z_in = 3 - z
    low = z // 2
    planes = [z, z_near, 2 - low, 3 - 3 * low]
    xdev, ydev = dev(z, 0, 1), dev(z, 1, 0)

    def remote(src, dst, ss, rs, target):
        return pltpu.make_async_remote_copy(
            src_ref=src, dst_ref=dst, send_sem=ss, recv_sem=rs,
            device_id={"vocab": target}, device_id_type=pl.DeviceIdType.MESH)

    def partner(src, dst, i):
        return pltpu.make_async_remote_copy(
            src_ref=src, dst_ref=dst, send_sem=p_send.at[i], recv_sem=p_recv.at[i],
            device_id={"rows": 1 - core}, device_id_type=pl.DeviceIdType.MESH)

    cp_w = pltpu.make_async_copy(w_hbm, w, loc_sem.at[0])
    cp_w.start()
    gath[me] = h_ref[...]

    barrier = pltpu.get_barrier_semaphore()

    def greet(i, c):
        pl.semaphore_signal(barrier, inc=1, device_id={"vocab": lax.rem(me + i, n)},
                            device_id_type=pl.DeviceIdType.MESH)
        return c
    lax.fori_loop(1, n, greet, 0)
    pl.semaphore_signal(barrier, inc=1, device_id={"rows": 1 - core},
                        device_id_type=pl.DeviceIdType.MESH)
    pl.semaphore_wait(barrier, n)

    def gcopy(slot, h, ss, target):
        ref = gath.at[slot] if h is None else gath.at[slot, pl.ds(h * half, half)]
        return remote(ref, ref, ss, ag_recv.at[slot, h or 0], target)

    def wait_piece(slot, h=None):
        gcopy(slot, h, f_send.at[0, 0], xdev).wait_recv()

    pending, pending_mid = [], []

    def go(c):
        c.start()
        pending.append(c)

    def go_mid(c):
        pl.when(mid)(c.start)
        pending_mid.append(c)

    def fan_out(i):
        slot = dev(planes[i], 0, 0)
        go(gcopy(slot, None, xy_send.at[i, 0], ydev))
        go(gcopy(slot, None, xy_send.at[i, 1], xdev))

    def forward(i):
        s0, s1 = dev(planes[i], 1, 0), dev(planes[i], 0, 1)
        wait_piece(s0)
        go(gcopy(s0, 0, f_send.at[i, 0], xdev))
        if i == 0:
            go(gcopy(s0, None, xy_send.at[1, 0], zn_dev))
        wait_piece(s1)
        go(gcopy(s1, 1, f_send.at[i, 1], ydev))
        if i == 0:
            go(gcopy(s1, None, xy_send.at[1, 1], zn_dev))

    def wrows(slot, count):
        return pl.ds(pl.multiple_of(slot * width, width), count * width)

    def multiply(slot, count, first=False):
        a = jnp.concatenate([gath[slot + c] for c in range(count)], axis=1)
        part = jnp.dot(a, w[wrows(slot, count), :], preferred_element_type=f32)
        if first:
            es[...] = part
        else:
            es[...] += part

    def plane(i):
        s = dev(planes[i], 1, 1)
        if i == 3:
            multiply(planes[3] * 4 + 2 * y, 2)
        wait_piece(s, 0)
        wait_piece(s, 1)
        if i == 3:
            multiply(planes[3] * 4 + 2 * (1 - y), 2)
        else:
            multiply(planes[i] * 4, 4, i == 0)

    zn_dev, zi_dev = dev(z_near, 0, 0), dev(z_in, 0, 0)
    go(gcopy(me, None, z_send.at[0], zn_dev))
    go_mid(gcopy(me, None, z_send.at[1], zi_dev))
    fan_out(0)

    block = 32
    nblk = tok // block
    lane = lax.broadcasted_iota(jnp.int32, (block, 128), 1)

    def teacher(b, c):
        rows = pl.ds(pl.multiple_of(b * block, block), block)
        tv = t[rows, :].astype(f32) / sharpness_divisor
        m = jnp.max(tv, axis=1, keepdims=True)
        e = jnp.exp(tv - m)
        et[rows, :] = e
        total = jnp.sum(e, axis=1, keepdims=True)
        cols[rows, :] = jnp.where(lane == 2, m, jnp.where(lane == 3, total, 0.0))
        return c
    lax.fori_loop(0, nblk, teacher, 0)

    for i in range(1, 4):
        slot = dev(planes[i], 0, 0)
        target = zi_dev if i == 1 else zn_dev
        wait_piece(slot)
        go_mid(gcopy(slot, None, z_send.at[1 + i], target))
        if i > 1:
            fan_out(i)
        forward(i - 1)
        if i > 1:
            if i == 2:
                cp_w.wait()
            plane(i - 2)
    forward(3)
    plane(2)
    plane(3)

    mine = n // 2
    ph = partner(gath.at[pl.ds((1 - core) * mine, mine)], pgath, 0)
    ph.start()

    def student(b, c):
        rows = pl.ds(pl.multiple_of(b * block, block), block)
        sv = es[rows, :] / sharpness_divisor
        tv = t[rows, :].astype(f32) / sharpness_divisor
        m = jnp.max(sv, axis=1, keepdims=True)
        e = jnp.exp(sv - m)
        es[rows, :] = e
        total = jnp.sum(e, axis=1, keepdims=True)
        weighted = jnp.sum(et[rows, :] * (tv - sv), axis=1, keepdims=True)
        old = cols[rows, :]
        cols[rows, :] = jnp.where(
            lane == 0, m, jnp.where(lane == 1, total, jnp.where(lane == 4, weighted, old)))
        return c
    lax.fori_loop(0, nblk, student, 0)
    stat[me] = jnp.transpose(cols[...])[:8, :]

    def stat_copy(i):
        return remote(stat.at[me], stat.at[me], st_send.at[i], st_recv.at[me],
                      lax.rem(me + i, n))

    def stat_start(i, c):
        stat_copy(i).start()
        return c
    lax.fori_loop(1, n, stat_start, 0)

    def stat_wait(i, c):
        other = lax.rem(me + i, n)
        remote(stat.at[other], stat.at[other], st_send.at[i], st_recv.at[other],
               other).wait_recv()
        return c
    lax.fori_loop(1, n, stat_wait, 0)

    ms, ss = stat[:, 0:1, :], stat[:, 1:2, :]
    mt, tt, wt = stat[:, 2:3, :], stat[:, 3:4, :], stat[:, 4:5, :]
    top_s, top_t = jnp.max(ms, axis=0), jnp.max(mt, axis=0)
    total_s = jnp.sum(ss * jnp.exp(ms - top_s[None]), axis=0)
    scale_t = jnp.exp(mt - top_t[None])
    total_t = jnp.sum(tt * scale_t, axis=0)
    cross = jnp.sum(wt * scale_t, axis=0) / total_t
    lse_s = top_s + jnp.log(total_s)
    lse_t = top_t + jnp.log(total_t)
    mm_ref[...] = sharpness_divisor * sharpness_divisor * (cross + lse_s - lse_t)
    own = stat[me]
    gain = objective_factor * sharpness_divisor
    rowsbuf[...] = jnp.zeros_like(rowsbuf)
    rowsbuf[0:1, :] = gain * jnp.exp(own[0:1, :] - lse_s)
    rowsbuf[1:2, :] = gain * jnp.exp(own[2:3, :] - lse_t)
    cols[...] = jnp.transpose(rowsbuf[...])

    def derive(b, c):
        rows = pl.ds(pl.multiple_of(b * block, block), block)
        f = cols[rows, :]
        score[rows, :] = (es[rows, :] * f[:, 0:1] - et[rows, :] * f[:, 1:2]).astype(bf16)
        return c
    lax.fori_loop(0, nblk, derive, 0)
    ps = partner(score.at[pl.ds(0, tok)], score.at[pl.ds(tok, tok)], 1)
    ps.start()

    order = [planes[3], planes[2], planes[1], planes[0]]

    def block_of(dy, dx):
        slot = dev(0, dy, dx)
        return pl.ds(pl.multiple_of(slot * width, width), width)

    near, beside, across, diag = block_of(0, 0), block_of(1, 0), block_of(0, 1), block_of(1, 1)
    top, bottom = pl.ds(0, half), pl.ds(half, half)

    def xcopy(k):
        return remote(sx.at[k], rx.at[k], x_send.at[k], x_recv.at[k], xdev)

    def ycopy(k):
        return remote(sy.at[k], ry.at[k], y_send.at[k], y_recv.at[k], ydev)

    def jcopy(k, d):
        return remote(sj.at[k, d], rj.at[k, d], j_send.at[k, d], j_recv.at[k, d],
                      xdev if d else ydev)

    def xdiag(k):
        return remote(sx.at[k, 0], rx.at[k, 0], x_send.at[k], x_recv.at[k], xdev)

    def ydiag(k):
        return remote(sy.at[k, 0], ry.at[k, 0], y_send.at[k], y_recv.at[k], ydev)

    def ncopy(d):
        return remote(sn.at[0, d], rn.at[0, d], n_send.at[0, d], n_recv.at[0, d], zn_dev)

    def fcopy(d):
        return remote(sn.at[1, d], rn.at[1, d], n_send.at[1, d], n_recv.at[1, d],
                      xdev if d else ydev)

    def home(k):
        sd[k] = pp[k, :, near].astype(bf16)
        go(remote(sd.at[k], rd.at[z], d_send.at[k], d_recv.at[z], dev(order[k], 0, 0)))

    for k in (2, 3, 0, 1):
        pp[k] = lax.dot_general(score[:tok, :], w[wrows(order[k] * 4, 4), :], NT,
                                preferred_element_type=f32)
        sx[k, 0] = pp[k, top, diag].astype(bf16)
        sy[k, 0] = pp[k, bottom, diag].astype(bf16)
        if k < 2:
            sx[k, 1] = pp[k, top, across].astype(bf16)
            sy[k, 1] = pp[k, bottom, beside].astype(bf16)
            go(xcopy(k))
            go(ycopy(k))
        else:
            go(xdiag(k))
            go(ydiag(k))

    def whole(k, i, copy):
        xdiag(k).wait_recv()
        sn[i, 0, top, :] = (pp[k, top, beside] + rx[k, 0].astype(f32)).astype(bf16)
        sn[i, 0, bottom, :] = pp[k, bottom, beside].astype(bf16)
        go(copy(0))
        ydiag(k).wait_recv()
        sn[i, 1, top, :] = pp[k, top, across].astype(bf16)
        sn[i, 1, bottom, :] = (pp[k, bottom, across] + ry[k, 0].astype(f32)).astype(bf16)
        go(copy(1))

    pair = 2

    def weight_part(j, c):
        slot = core * mine + j * pair
        a = jnp.concatenate(
            [jnp.concatenate([gath[slot + i], pgath[j * pair + i]], axis=0) for i in range(pair)],
            axis=1)
        for v in range(2):
            vs = pl.ds(v * (w.shape[1] // 2), w.shape[1] // 2)
            g = lax.dot_general(a, score[:, vs], TN, preferred_element_type=f32)
            wg_ref[pl.ds(pl.multiple_of(j * pair * width, width), pair * width), vs] = g.astype(bf16)
        return c

    def join(k):
        xcopy(k).wait_recv()
        sj[k, 0] = (pp[k, top, beside] + rx[k, 0].astype(f32)).astype(bf16)
        go(jcopy(k, 0))
        ycopy(k).wait_recv()
        sj[k, 1] = (pp[k, bottom, across] + ry[k, 0].astype(f32)).astype(bf16)
        go(jcopy(k, 1))

    def column(k):
        jcopy(k, 0).wait_recv()
        pp[k, top, near] += rj[k, 0].astype(f32) + rx[k, 1].astype(f32)
        jcopy(k, 1).wait_recv()
        pp[k, bottom, near] += rj[k, 1].astype(f32) + ry[k, 1].astype(f32)
        home(k)

    chunks = mine // pair

    def wait_partner():
        ph.wait()
        ps.wait()

    whole(2, 0, ncopy)
    join(0)
    join(1)
    home(2)
    pl.when(core == 0)(wait_partner)
    lax.fori_loop(0, (1 - core) * (chunks // 2), weight_part, 0)
    ncopy(0).wait_recv()
    pp[3, :, beside] += rn[0, 0].astype(f32)
    ncopy(1).wait_recv()
    pp[3, :, across] += rn[0, 1].astype(f32)
    whole(3, 1, fcopy)
    column(0)
    column(1)
    lax.fori_loop((1 - core) * (chunks // 2), (1 - core) * chunks, weight_part, 0)
    pl.when(core == 1)(wait_partner)
    lax.fori_loop(0, core * chunks, weight_part, 0)
    fcopy(0).wait_recv()
    fcopy(1).wait_recv()
    pp[3, :, near] += rn[1, 0].astype(f32) + rn[1, 1].astype(f32)
    total = pp[3, :, near]
    for k in range(3):
        zz = order[k]
        remote(sd.at[k], rd.at[zz], d_send.at[k], d_recv.at[zz], dev(zz, 0, 0)).wait_recv()
        total += rd[zz].astype(f32)
    hg_ref[...] = total.astype(bf16)

    for c in pending:
        c.wait_send()

    @pl.when(mid)
    def _():
        for c in pending_mid:
            c.wait_send()

    def stat_done(i, c):
        stat_copy(i).wait_send()
        return c
    lax.fori_loop(1, n, stat_done, 0)

def fused(n, hidden, head_weight, mentor_outputs):
    tok, width = hidden.shape
    feats, voc = head_weight.shape
    half, mine = tok // 2, n // 2
    vm = pltpu.VMEM
    dma = pltpu.SemaphoreType.DMA
    anyspace = pl.BlockSpec(memory_space=pl.ANY)
    vspace = pl.BlockSpec(memory_space=pltpu.VMEM)
    hg, wg, mm = pl.pallas_call(
        stages,
        out_shape=(
            jax.ShapeDtypeStruct((tok, width), bf16),
            jax.ShapeDtypeStruct((feats // 2, voc), bf16),
            jax.ShapeDtypeStruct((1, tok), f32),
        ),
        in_specs=[vspace, anyspace, vspace],
        out_specs=(vspace,) * 3,
        scratch_shapes=[
            vm((n, tok, width), bf16),
            vm((mine, tok, width), bf16),
            vm((feats, voc), bf16),
            vm((tok, voc), f32),
            vm((tok, voc), f32),
            vm((2 * tok, voc), bf16),
            vm((tok, 128), f32),
            vm((128, tok), f32),
            vm((n, 8, tok), f32),
            vm((4, 2, half, width), bf16),
            vm((4, 2, half, width), bf16),
            vm((4, 2, half, width), bf16),
            vm((4, 2, half, width), bf16),
            vm((4, 2, half, width), bf16),
            vm((4, 2, half, width), bf16),
            vm((2, 2, tok, width), bf16),
            vm((2, 2, tok, width), bf16),
            vm((4, tok, 4 * width), f32),
            vm((3, tok, width), bf16),
            vm((4, tok, width), bf16),
            dma((1,)),
            dma((n, 2)),
            dma((5,)),
            dma((4, 2)),
            dma((4, 2)),
            dma((n,)),
            dma((n,)),
            dma((4,)),
            dma((4,)),
            dma((4,)),
            dma((4,)),
            dma((4, 2)),
            dma((4, 2)),
            dma((2, 2)),
            dma((2, 2)),
            dma((3,)),
            dma((4,)),
            dma((2,)),
            dma((2,)),
        ],
        compiler_params=pltpu.CompilerParams(
            collective_id=0, has_side_effects=True, vmem_limit_bytes=48 * 1024 * 1024),
        cost_estimate=pl.CostEstimate(
            flops=6 * tok * feats * voc, transcendentals=2 * tok * voc,
            bytes_accessed=2 * feats * voc + feats * voc),
    )(hidden, head_weight, mentor_outputs)
    return hg, wg, mm.reshape(tok)


def collective(hidden, head_weight, mentor_outputs):
    full_hidden = lax.all_gather(hidden, "vocab", axis=1, tiled=True)
    student = jnp.dot(full_hidden, head_weight, preferred_element_type=f32) / sharpness_divisor
    target = mentor_outputs.astype(f32) / sharpness_divisor
    top_s, top_t = lax.pmax((jnp.max(student, axis=1), jnp.max(target, axis=1)), "vocab")
    exp_s = jnp.exp(student - top_s[:, None])
    exp_t = jnp.exp(target - top_t[:, None])
    total_s, total_t, weighted = lax.psum(
        (jnp.sum(exp_s, axis=1), jnp.sum(exp_t, axis=1),
         jnp.sum(exp_t * (target - student), axis=1)), "vocab")
    lse_s = top_s + jnp.log(total_s)
    lse_t = top_t + jnp.log(total_t)
    mismatch = sharpness_divisor * sharpness_divisor * (weighted / total_t + lse_s - lse_t)
    score = (objective_factor * sharpness_divisor
             * (jnp.exp(student - lse_s[:, None]) - jnp.exp(target - lse_t[:, None]))).astype(bf16)
    hidden_part = lax.psum_scatter(
        lax.dot_general(head_weight, score, NT, preferred_element_type=f32),
        "vocab", scatter_dimension=0, tiled=True)
    weight_grad = lax.psum_scatter(
        lax.dot_general(full_hidden, score, TN, preferred_element_type=f32),
        "rows", scatter_dimension=0, tiled=True).astype(bf16)
    return hidden_part.T.astype(bf16), weight_grad, mismatch


def solution(mesh):
    n = mesh.shape["vocab"]

    def shards(hidden, head_weight, mentor_outputs):
        if n == 16 and mesh.shape["rows"] == 2 and hidden.shape[1] % 128 == 0:
            return fused(n, hidden, head_weight, mentor_outputs)
        return collective(hidden, head_weight, mentor_outputs)

    return jax.shard_map(
        shards,
        mesh=mesh,
        in_specs=(P("rows", "vocab"), P(None, "vocab"), P("rows", "vocab")),
        out_specs=(P("rows", "vocab"), P("rows", "vocab"), P("rows")),
        check_vma=False,
    )
```

```python
import functools

import jax
import jax.numpy as jnp
from jax import lax
from jax.experimental import pallas as pl
from jax.experimental.pallas import tpu as pltpu
from jax.sharding import PartitionSpec as P

sharpness_divisor = 2.0
objective_factor = 32.0
f32 = jnp.float32
bf16 = jnp.bfloat16

NT = (((1,), (1,)), ((), ()))
TN = (((0,), (0,)), ((), ()))


def stages(h_ref, w_hbm, t, hg_ref, wg_ref, mm_ref,
           gath, pgath, w, es, et, score, cols, rowsbuf, stat,
           sx, rx, sy, ry, sj, rj, pp, sd, rd, zb,
           loc_sem, ag_recv, z_send, xy_send, f_send, st_send, st_recv,
           x_send, x_recv, y_send, y_recv, j_send, j_recv, d_send, d_recv, e_send, e_recv, p_send, p_recv):
    n = gath.shape[0]
    tok, width = h_ref.shape
    half = tok // 2
    me = lax.axis_index("vocab")
    core = lax.axis_index("rows")
    z, y, x = me // 4, lax.rem(me // 2, 2), lax.rem(me, 2)
    mid = jnp.logical_or(z == 1, z == 2)

    def dev(zz, dy, dx):
        yy = 1 - y if dy else y
        xx = 1 - x if dx else x
        return zz * 4 + yy * 2 + xx

    z_near = z + 1 - 2 * lax.rem(z, 2)
    z_in = 3 - z
    low = z // 2
    planes = [z, z_near, 2 - low, 3 - 3 * low]
    xdev, ydev = dev(z, 0, 1), dev(z, 1, 0)

    def remote(src, dst, ss, rs, target):
        return pltpu.make_async_remote_copy(
            src_ref=src, dst_ref=dst, send_sem=ss, recv_sem=rs,
            device_id={"vocab": target}, device_id_type=pl.DeviceIdType.MESH)

    def partner(src, dst, i):
        return pltpu.make_async_remote_copy(
            src_ref=src, dst_ref=dst, send_sem=p_send.at[i], recv_sem=p_recv.at[i],
            device_id={"rows": 1 - core}, device_id_type=pl.DeviceIdType.MESH)

    cp_w = pltpu.make_async_copy(w_hbm, w, loc_sem.at[0])
    cp_w.start()
    gath[me] = h_ref[...]

    barrier = pltpu.get_barrier_semaphore()

    def greet(i, c):
        pl.semaphore_signal(barrier, inc=1, device_id={"vocab": lax.rem(me + i, n)},
                            device_id_type=pl.DeviceIdType.MESH)
        return c
    lax.fori_loop(1, n, greet, 0)
    pl.semaphore_signal(barrier, inc=1, device_id={"rows": 1 - core},
                        device_id_type=pl.DeviceIdType.MESH)
    pl.semaphore_wait(barrier, n)

    def gcopy(slot, h, ss, target):
        ref = gath.at[slot] if h is None else gath.at[slot, pl.ds(h * half, half)]
        return remote(ref, ref, ss, ag_recv.at[slot, h or 0], target)

    def wait_piece(slot, h=None):
        gcopy(slot, h, f_send.at[0, 0], xdev).wait_recv()

    pending, pending_mid = [], []

    def go(c):
        c.start()
        pending.append(c)

    def go_mid(c):
        pl.when(mid)(c.start)
        pending_mid.append(c)

    def fan_out(i):
        slot = dev(planes[i], 0, 0)
        go(gcopy(slot, None, xy_send.at[i, 0], ydev))
        go(gcopy(slot, None, xy_send.at[i, 1], xdev))

    def forward(i):
        s0, s1 = dev(planes[i], 1, 0), dev(planes[i], 0, 1)
        wait_piece(s0)
        go(gcopy(s0, 0, f_send.at[i, 0], xdev))
        wait_piece(s1)
        go(gcopy(s1, 1, f_send.at[i, 1], ydev))

    def wrows(slot, count):
        return pl.ds(pl.multiple_of(slot * width, width), count * width)

    def multiply(slot, count, first=False):
        a = jnp.concatenate([gath[slot + c] for c in range(count)], axis=1)
        part = jnp.dot(a, w[wrows(slot, count), :], preferred_element_type=f32)
        if first:
            es[...] = part
        else:
            es[...] += part

    def plane(i):
        s = dev(planes[i], 1, 1)
        if i == 3:
            multiply(planes[3] * 4 + 2 * y, 2)
        wait_piece(s, 0)
        wait_piece(s, 1)
        if i == 3:
            multiply(planes[3] * 4 + 2 * (1 - y), 2)
        else:
            multiply(planes[i] * 4, 4, i == 0)

    zn_dev, zi_dev = dev(z_near, 0, 0), dev(z_in, 0, 0)
    go(gcopy(me, None, z_send.at[0], zn_dev))
    go_mid(gcopy(me, None, z_send.at[1], zi_dev))
    fan_out(0)

    block = 32
    nblk = tok // block
    lane = lax.broadcasted_iota(jnp.int32, (block, 128), 1)

    def teacher(b, c):
        rows = pl.ds(pl.multiple_of(b * block, block), block)
        tv = t[rows, :].astype(f32) / sharpness_divisor
        m = jnp.max(tv, axis=1, keepdims=True)
        e = jnp.exp(tv - m)
        et[rows, :] = e
        total = jnp.sum(e, axis=1, keepdims=True)
        cols[rows, :] = jnp.where(lane == 2, m, jnp.where(lane == 3, total, 0.0))
        return c
    lax.fori_loop(0, nblk, teacher, 0)

    for i in range(1, 4):
        slot = dev(planes[i], 0, 0)
        target = zi_dev if i == 1 else zn_dev
        wait_piece(slot)
        go_mid(gcopy(slot, None, z_send.at[1 + i], target))
        fan_out(i)
        forward(i - 1)
        if i > 1:
            if i == 2:
                cp_w.wait()
            plane(i - 2)
    forward(3)
    plane(2)
    plane(3)

    mine = n // 2
    ph = partner(gath.at[pl.ds((1 - core) * mine, mine)], pgath, 0)
    ph.start()

    def student(b, c):
        rows = pl.ds(pl.multiple_of(b * block, block), block)
        sv = es[rows, :] / sharpness_divisor
        tv = t[rows, :].astype(f32) / sharpness_divisor
        m = jnp.max(sv, axis=1, keepdims=True)
        e = jnp.exp(sv - m)
        es[rows, :] = e
        total = jnp.sum(e, axis=1, keepdims=True)
        weighted = jnp.sum(et[rows, :] * (tv - sv), axis=1, keepdims=True)
        old = cols[rows, :]
        cols[rows, :] = jnp.where(
            lane == 0, m, jnp.where(lane == 1, total, jnp.where(lane == 4, weighted, old)))
        return c
    lax.fori_loop(0, nblk, student, 0)
    stat[me] = jnp.transpose(cols[...])[:8, :]

    def stat_copy(i):
        return remote(stat.at[me], stat.at[me], st_send.at[i], st_recv.at[me],
                      lax.rem(me + i, n))

    def stat_start(i, c):
        stat_copy(i).start()
        return c
    lax.fori_loop(1, n, stat_start, 0)

    def stat_wait(i, c):
        other = lax.rem(me + i, n)
        remote(stat.at[other], stat.at[other], st_send.at[i], st_recv.at[other],
               other).wait_recv()
        return c
    lax.fori_loop(1, n, stat_wait, 0)

    ms, ss = stat[:, 0:1, :], stat[:, 1:2, :]
    mt, tt, wt = stat[:, 2:3, :], stat[:, 3:4, :], stat[:, 4:5, :]
    top_s, top_t = jnp.max(ms, axis=0), jnp.max(mt, axis=0)
    total_s = jnp.sum(ss * jnp.exp(ms - top_s[None]), axis=0)
    scale_t = jnp.exp(mt - top_t[None])
    total_t = jnp.sum(tt * scale_t, axis=0)
    cross = jnp.sum(wt * scale_t, axis=0) / total_t
    lse_s = top_s + jnp.log(total_s)
    lse_t = top_t + jnp.log(total_t)
    mm_ref[...] = sharpness_divisor * sharpness_divisor * (cross + lse_s - lse_t)
    own = stat[me]
    gain = objective_factor * sharpness_divisor
    rowsbuf[...] = jnp.zeros_like(rowsbuf)
    rowsbuf[0:1, :] = gain * jnp.exp(own[0:1, :] - lse_s)
    rowsbuf[1:2, :] = gain * jnp.exp(own[2:3, :] - lse_t)
    cols[...] = jnp.transpose(rowsbuf[...])

    def derive(b, c):
        rows = pl.ds(pl.multiple_of(b * block, block), block)
        f = cols[rows, :]
        score[rows, :] = (es[rows, :] * f[:, 0:1] - et[rows, :] * f[:, 1:2]).astype(bf16)
        return c
    lax.fori_loop(0, nblk, derive, 0)
    ps = partner(score.at[pl.ds(0, tok)], score.at[pl.ds(tok, tok)], 1)
    ps.start()

    order = [planes[3], planes[2], planes[1], planes[0]]

    def block_of(dy, dx):
        slot = dev(0, dy, dx)
        return pl.ds(pl.multiple_of(slot * width, width), width)

    near, beside, across, diag = block_of(0, 0), block_of(1, 0), block_of(0, 1), block_of(1, 1)
    top, bottom = pl.ds(0, half), pl.ds(half, half)

    def xcopy(k):
        return remote(sx.at[k], rx.at[k], x_send.at[k], x_recv.at[k], xdev)

    def ycopy(k):
        return remote(sy.at[k], ry.at[k], y_send.at[k], y_recv.at[k], ydev)

    def jcopy(k, d):
        return remote(sj.at[k, d], rj.at[k, d], j_send.at[k, d], j_recv.at[k, d],
                      xdev if d else ydev)

    for k in range(4):
        pp[k] = lax.dot_general(score[:tok, :], w[wrows(order[k] * 4, 4), :], NT,
                                preferred_element_type=f32)
        sx[k, 0] = pp[k, top, diag].astype(bf16)
        sx[k, 1] = pp[k, top, across].astype(bf16)
        go(xcopy(k))
        sy[k, 0] = pp[k, bottom, diag].astype(bf16)
        sy[k, 1] = pp[k, bottom, beside].astype(bf16)
        go(ycopy(k))

    pair = 2

    def weight_part(j, c):
        slot = core * mine + j * pair
        a = jnp.concatenate(
            [jnp.concatenate([gath[slot + i], pgath[j * pair + i]], axis=0) for i in range(pair)],
            axis=1)
        for v in range(2):
            vs = pl.ds(v * (w.shape[1] // 2), w.shape[1] // 2)
            g = lax.dot_general(a, score[:, vs], TN, preferred_element_type=f32)
            wg_ref[pl.ds(pl.multiple_of(j * pair * width, width), pair * width), vs] = g.astype(bf16)
        return c

    def join(k):
        xcopy(k).wait_recv()
        sj[k, 0] = (pp[k, top, beside] + rx[k, 0].astype(f32)).astype(bf16)
        go(jcopy(k, 0))
        ycopy(k).wait_recv()
        sj[k, 1] = (pp[k, bottom, across] + ry[k, 0].astype(f32)).astype(bf16)
        go(jcopy(k, 1))

    def dcopy(k):
        return remote(sd.at[k], rd.at[z], d_send.at[k], d_recv.at[z], dev(order[k], 0, 0))

    def ecopy(k):
        return remote(sd.at[k], zb.at[k], e_send.at[k], e_recv.at[k], zn_dev)

    def column(k):
        jcopy(k, 0).wait_recv()
        pp[k, top, near] += rj[k, 0].astype(f32) + rx[k, 1].astype(f32)
        jcopy(k, 1).wait_recv()
        pp[k, bottom, near] += rj[k, 1].astype(f32) + ry[k, 1].astype(f32)
        if k < 2:
            @pl.when(mid)
            def _():
                ecopy(k).wait_recv()
                pp[k, :, near] += zb[k].astype(f32)
        if k < 3:
            sd[k] = pp[k, :, near].astype(bf16)
        if k < 2:
            pl.when(mid)(dcopy(k).start)
            pl.when(jnp.logical_not(mid))(ecopy(k).start)
        elif k == 2:
            go(dcopy(k))

    chunks = mine // pair

    def wait_partner():
        ph.wait()
        ps.wait()

    join(0)
    join(1)
    pl.when(core == 0)(wait_partner)
    lax.fori_loop(0, (1 - core) * (chunks // 2), weight_part, 0)
    join(2)
    join(3)
    column(0)
    lax.fori_loop((1 - core) * (chunks // 2), (1 - core) * chunks, weight_part, 0)
    column(1)
    column(2)
    pl.when(core == 1)(wait_partner)
    lax.fori_loop(0, core * chunks, weight_part, 0)
    column(3)
    total = pp[3, :, near]
    for k in range(1, 3):
        zz = order[k]
        remote(sd.at[k], rd.at[zz], d_send.at[k], d_recv.at[zz], dev(zz, 0, 0)).wait_recv()
        total += rd[zz].astype(f32)
    hg_ref[...] = total.astype(bf16)

    for c in pending:
        c.wait_send()

    @pl.when(mid)
    def _():
        for c in pending_mid:
            c.wait_send()
        for k in range(2):
            dcopy(k).wait_send()

    @pl.when(jnp.logical_not(mid))
    def _():
        for k in range(2):
            ecopy(k).wait_send()

    def stat_done(i, c):
        stat_copy(i).wait_send()
        return c
    lax.fori_loop(1, n, stat_done, 0)

def fused(n, hidden, head_weight, mentor_outputs):
    tok, width = hidden.shape
    feats, voc = head_weight.shape
    half, mine = tok // 2, n // 2
    vm = pltpu.VMEM
    dma = pltpu.SemaphoreType.DMA
    anyspace = pl.BlockSpec(memory_space=pl.ANY)
    vspace = pl.BlockSpec(memory_space=pltpu.VMEM)
    hg, wg, mm = pl.pallas_call(
        stages,
        out_shape=(
            jax.ShapeDtypeStruct((tok, width), bf16),
            jax.ShapeDtypeStruct((feats // 2, voc), bf16),
            jax.ShapeDtypeStruct((1, tok), f32),
        ),
        in_specs=[vspace, anyspace, vspace],
        out_specs=(vspace,) * 3,
        scratch_shapes=[
            vm((n, tok, width), bf16),
            vm((mine, tok, width), bf16),
            vm((feats, voc), bf16),
            vm((tok, voc), f32),
            vm((tok, voc), f32),
            vm((2 * tok, voc), bf16),
            vm((tok, 128), f32),
            vm((128, tok), f32),
            vm((n, 8, tok), f32),
            vm((4, 2, half, width), bf16),
            vm((4, 2, half, width), bf16),
            vm((4, 2, half, width), bf16),
            vm((4, 2, half, width), bf16),
            vm((4, 2, half, width), bf16),
            vm((4, 2, half, width), bf16),
            vm((4, tok, 4 * width), f32),
            vm((3, tok, width), bf16),
            vm((4, tok, width), bf16),
            vm((2, tok, width), bf16),
            dma((1,)),
            dma((n, 2)),
            dma((5,)),
            dma((4, 2)),
            dma((4, 2)),
            dma((n,)),
            dma((n,)),
            dma((4,)),
            dma((4,)),
            dma((4,)),
            dma((4,)),
            dma((4, 2)),
            dma((4, 2)),
            dma((3,)),
            dma((4,)),
            dma((2,)),
            dma((2,)),
            dma((2,)),
            dma((2,)),
        ],
        compiler_params=pltpu.CompilerParams(
            collective_id=0, has_side_effects=True, vmem_limit_bytes=48 * 1024 * 1024),
        cost_estimate=pl.CostEstimate(
            flops=6 * tok * feats * voc, transcendentals=2 * tok * voc,
            bytes_accessed=2 * feats * voc + feats * voc),
    )(hidden, head_weight, mentor_outputs)
    return hg, wg, mm.reshape(tok)


def collective(hidden, head_weight, mentor_outputs):
    full_hidden = lax.all_gather(hidden, "vocab", axis=1, tiled=True)
    student = jnp.dot(full_hidden, head_weight, preferred_element_type=f32) / sharpness_divisor
    target = mentor_outputs.astype(f32) / sharpness_divisor
    top_s, top_t = lax.pmax((jnp.max(student, axis=1), jnp.max(target, axis=1)), "vocab")
    exp_s = jnp.exp(student - top_s[:, None])
    exp_t = jnp.exp(target - top_t[:, None])
    total_s, total_t, weighted = lax.psum(
        (jnp.sum(exp_s, axis=1), jnp.sum(exp_t, axis=1),
         jnp.sum(exp_t * (target - student), axis=1)), "vocab")
    lse_s = top_s + jnp.log(total_s)
    lse_t = top_t + jnp.log(total_t)
    mismatch = sharpness_divisor * sharpness_divisor * (weighted / total_t + lse_s - lse_t)
    score = (objective_factor * sharpness_divisor
             * (jnp.exp(student - lse_s[:, None]) - jnp.exp(target - lse_t[:, None]))).astype(bf16)
    hidden_part = lax.psum_scatter(
        lax.dot_general(head_weight, score, NT, preferred_element_type=f32),
        "vocab", scatter_dimension=0, tiled=True)
    weight_grad = lax.psum_scatter(
        lax.dot_general(full_hidden, score, TN, preferred_element_type=f32),
        "rows", scatter_dimension=0, tiled=True).astype(bf16)
    return hidden_part.T.astype(bf16), weight_grad, mismatch


def solution(mesh):
    n = mesh.shape["vocab"]

    def shards(hidden, head_weight, mentor_outputs):
        if n == 16 and mesh.shape["rows"] == 2 and hidden.shape[1] % 128 == 0:
            return fused(n, hidden, head_weight, mentor_outputs)
        return collective(hidden, head_weight, mentor_outputs)

    return jax.shard_map(
        shards,
        mesh=mesh,
        in_specs=(P("rows", "vocab"), P(None, "vocab"), P("rows", "vocab")),
        out_specs=(P("rows", "vocab"), P("rows", "vocab"), P("rows")),
        check_vma=False,
    )
```
